256 devices in a mesh: ctx: 64 (over z, y, core), head: 4 (over x).
Axes of the slice: x: 4, y: 4, z: 8, core: 2. Of those that a mesh axis runs over, the one named last changes fastest.
Arguments:
- queries: bfloat16 [131072, 2048], P('ctx', 'head'), may hold values from -6 to 6
- keys: bfloat16 [131072, 2048], P('ctx', 'head'), may hold values from -6 to 6
- values: bfloat16 [131072, 2048], P('ctx', 'head'), may hold values from -6 to 6
- out_weight: bfloat16 [2048, 2048], P('head'), may hold values from -0.5 to 0.5
- block_order: int32 [1024], replicated, may hold values from 0 to 1023, as said below
- selection: int32 [1024, 2], P('ctx'), may hold values from 0 to 1023, as said below
Outputs:
- layer_out: bfloat16 [131072, 2048], P('ctx', 'head')
The draws below stay inside these ranges and needn't reach their ends.
Inputs may be any that keep to these rules, and one draw needn't show every extreme that they name: `block_order`: A permutation of the sequence's blocks; device d of ctx stores blocks d*16 to (d+1)*16 - 1. `selection`: for the stored block s with g = block_order[s], each entry is a sequence block before g, or g itself for an empty entry; the two entries of a row differ unless empty. Over the rows of one device, at most 1 entries that are not empty name blocks stored on any one device. Sequence block 0 is named by a row of every device. The row of sequence block 1023 has an empty second entry.
All inputs are finite; a program needn't handle non-finite values.
Results may differ from the reference program's by a relative error of at most 0.029.
Values may be sent and summed in bfloat16 or wider, within the bound.
A program may use at most 192 MiB of HBM per device.

```python
import jax
import jax.numpy as jnp
from jax import lax

D = 2048
DH = 128
BLK = 128
HD = 2048
BLOCKS_PER_SHARD = 16
TOKENS = 131072
N_CTX = 64
N_HEAD = 4


def shared_normal(key):
    return jax.random.truncated_normal(key, -6.0, 6.0, (TOKENS, HD), jnp.float32)


def draw_keys(key, part):
    base = shared_normal(key)
    return base.astype(jnp.bfloat16)


def draw_queries(key, part):
    key = jax.random.fold_in(key, 2)
    fresh = jax.random.truncated_normal(key, -6.0, 6.0, (TOKENS, HD), jnp.float32)
    return fresh.astype(jnp.bfloat16)


def pick_block(candidates, scores, valid, fallback):
    masked = jnp.where(valid, scores, -1)
    best = jnp.argmax(masked, axis=-1)
    chosen = jnp.take_along_axis(candidates, best[..., None], axis=-1)[..., 0]
    return jnp.where(jnp.any(valid, axis=-1), chosen, fallback)


def block_plan(key):
    total_blocks = BLOCKS_PER_SHARD * N_CTX
    item_count = 2 * BLOCKS_PER_SHARD
    capacity = max(1, item_count // N_CTX)
    key_order, key_targets, leading_key, runner_key = jax.random.split(jax.random.fold_in(key, 11), 4)
    block_order = jax.random.permutation(key_order, total_blocks).astype(jnp.int32)
    storage_of = jnp.zeros((total_blocks,), jnp.int32).at[block_order].set(jnp.arange(total_blocks, dtype=jnp.int32))
    ids_here = block_order.reshape(N_CTX, BLOCKS_PER_SHARD)
    owner_list = jnp.repeat(jnp.arange(N_CTX, dtype=jnp.int32), capacity)

    def shuffle(one_key):
        return jax.random.permutation(one_key, owner_list)
    shuffled = jax.vmap(shuffle)(jax.random.split(key_targets, N_CTX))
    popular_block_holder = storage_of[0] // BLOCKS_PER_SHARD
    hot_block = jnp.argmax(ids_here, axis=1).astype(jnp.int32)

    def place_hot(owner_row, spot):
        found = jnp.argmax(owner_row == popular_block_holder)
        moved = owner_row[spot]
        return owner_row.at[found].set(moved).at[spot].set(popular_block_holder)
    targets = jax.vmap(place_hot)(shuffled, 2 * hot_block)[:, :item_count].reshape(N_CTX, BLOCKS_PER_SHARD, 2)
    candidates = ids_here[targets]
    own_ids = ids_here[:, :, None]
    score_boost = jnp.arange(BLOCKS_PER_SHARD, dtype=jnp.int32)
    leading_score = jax.random.randint(leading_key, (N_CTX, BLOCKS_PER_SHARD, BLOCKS_PER_SHARD), 0, 1 << 20) * BLOCKS_PER_SHARD + score_boost
    runner_score = jax.random.randint(runner_key, (N_CTX, BLOCKS_PER_SHARD, BLOCKS_PER_SHARD), 0, 1 << 20) * BLOCKS_PER_SHARD + score_boost
    first_ok = candidates[:, :, 0] < own_ids
    first_pick = pick_block(candidates[:, :, 0], leading_score, first_ok, ids_here)
    is_hot = jnp.arange(BLOCKS_PER_SHARD, dtype=jnp.int32)[None, :] == hot_block[:, None]
    first_pick = jnp.where(is_hot, 0, first_pick)
    second_ok = (candidates[:, :, 1] < own_ids) & (candidates[:, :, 1] != first_pick[:, :, None])
    second_pick = pick_block(candidates[:, :, 1], runner_score, second_ok, ids_here)
    second_pick = jnp.where(ids_here == total_blocks - 1, ids_here, second_pick)
    selection = jnp.stack([first_pick, second_pick], axis=-1).reshape(total_blocks, 2).astype(jnp.int32)
    return (block_order, selection)


def draw_block_order(key, part):
    return block_plan(key)[0]


def draw_selection(key, part):
    return block_plan(key)[1]


def level_of(rng, extent, cuts, least, largest):
    level, own = 1.0, jax.random.fold_in(rng, 6)
    for dim, parts in cuts:
        draws = jnp.exp(jax.random.uniform(jax.random.fold_in(own, dim), (parts,), jnp.float32, least / len(cuts), largest / len(cuts)))
        level = level * jnp.repeat(draws, extent[dim] // parts).reshape([-1 if axis == dim else 1 for axis in range(len(extent))])
    return level


def noise(stream_key, shape, spread, reach, shards=(), kind=jnp.bfloat16):
    level = level_of(stream_key, shape, shards, -0.22, 0.18) if shards else 1.0
    drawn = jax.random.normal(stream_key, shape, jnp.float32) * spread * level
    return jnp.minimum(jnp.maximum(drawn, -reach), reach).astype(kind)


def setup_inputs(seed: int = 0) -> dict:
    arg_keys = jax.random.split(jax.random.key(seed), 7)
    return {
        "queries": draw_queries(jax.random.fold_in(arg_keys[6], 71), 0),
        "keys": draw_keys(jax.random.fold_in(arg_keys[6], 71), 0),
        "values": noise(arg_keys[2], (TOKENS, HD), 1.0, 6.0, ((0, 64), (1, 4))),
        "out_weight": noise(arg_keys[3], (HD, D), (HD // 16) ** -0.5, 0.5, ((0, 4),)),
        "block_order": draw_block_order(jax.random.fold_in(arg_keys[6], 71), 0),
        "selection": draw_selection(jax.random.fold_in(arg_keys[6], 71), 0),
    }


NEG_BIG = -1e30


def attend_block(query_rows, key_rows, value_rows, allowed):
    block_rows = query_rows.shape[0]
    head_count = query_rows.shape[1] // DH
    q_split = query_rows.astype(jnp.float32).reshape(block_rows, head_count, DH)
    k_split = key_rows.astype(jnp.float32).reshape(block_rows, head_count, DH)
    v_split = value_rows.astype(jnp.float32).reshape(block_rows, head_count, DH)
    scores = jnp.einsum("qhd,khd->hqk", q_split, k_split) * (DH ** -0.5)
    scores = jnp.where(allowed, scores, NEG_BIG)
    row_max = jnp.max(scores, axis=-1, keepdims=True)
    weights = jnp.exp(scores - row_max)
    totals = jnp.sum(weights, axis=-1)
    rounded = lax.optimization_barrier(weights.astype(jnp.bfloat16)).astype(jnp.float32)
    mixed_out = jnp.einsum("hqk,khd->qhd", rounded, v_split)
    mixed_out = mixed_out / jnp.swapaxes(totals, 0, 1)[:, :, None]
    log_total = row_max[:, :, 0] + jnp.log(totals)
    return mixed_out.reshape(block_rows, head_count * DH), log_total


def spread_heads(weight_map):
    return jnp.repeat(jnp.swapaxes(weight_map, -1, -2), DH, axis=-1)


def combine_parts(own_out, own_log, item_out, item_log, live):
    live_mask = live[:, :, None, None] != 0
    live_log = jnp.where(live_mask, item_log, own_log[:, None])
    row_max = jnp.maximum(own_log, jnp.max(live_log, axis=1))
    own_weight = jnp.exp(own_log - row_max)
    item_weight = jnp.where(live_mask, jnp.exp(live_log - row_max[:, None]), 0.0)
    total = own_weight + jnp.sum(item_weight, axis=1)
    merged = spread_heads(own_weight) * own_out
    merged = merged + jnp.sum(spread_heads(item_weight) * item_out.astype(jnp.float32), axis=1)
    return (merged / spread_heads(total)).astype(jnp.bfloat16)


def reference(queries, keys, values, out_weight, block_order, selection):
    total_blocks = BLOCKS_PER_SHARD * N_CTX
    storage_of = jnp.zeros((total_blocks,), jnp.int32).at[block_order].set(jnp.arange(total_blocks, dtype=jnp.int32))
    q_blocks = queries.reshape(total_blocks, BLK, HD)
    k_blocks = keys.reshape(total_blocks, BLK, HD)
    v_blocks = values.reshape(total_blocks, BLK, HD)
    causal = lax.broadcasted_iota(jnp.int32, (BLK, BLK), 0) >= lax.broadcasted_iota(jnp.int32, (BLK, BLK), 1)

    def one_block(index):
        own_out, own_log = attend_block(q_blocks[index], k_blocks[index], v_blocks[index], causal)
        picks = selection[index]
        slots = storage_of[picks]
        out_list = []
        log_list = []
        for which in range(2):
            part_out, part_log = attend_block(q_blocks[index], k_blocks[slots[which]], v_blocks[slots[which]], True)
            out_list.append(part_out.astype(jnp.bfloat16))
            log_list.append(part_log)
        item_out = jnp.stack(out_list)[None]
        item_log = jnp.stack(log_list)[None]
        live = (picks != block_order[index]).astype(jnp.int32)[None]
        return combine_parts(own_out[None], own_log[None], item_out, item_log, live)[0]

    attention_layer = lax.map(one_block, jnp.arange(total_blocks, dtype=jnp.int32)).reshape(TOKENS, HD)
    group_width = HD // N_HEAD
    summed = jnp.zeros((TOKENS, D), jnp.float32)
    for group in range(N_HEAD):
        part = jnp.dot(attention_layer[:, group * group_width:(group + 1) * group_width], out_weight[group * group_width:(group + 1) * group_width], preferred_element_type=jnp.float32)
        summed = summed + lax.optimization_barrier(part.astype(jnp.bfloat16)).astype(jnp.float32)
    return summed.astype(jnp.bfloat16)
```

```python
import functools

import jax
import jax.numpy as jnp
from jax import lax
from jax.experimental import pallas as pl
from jax.experimental.pallas import tpu as pltpu
from jax.sharding import PartitionSpec as P

MESH = pl.DeviceIdType.MESH
DH = 128
BLK = 128
HEADS = 4
BLOCKS = 16
ROWS = BLOCKS * BLK
PLANES = 8
MATES = 8
NZ = PLANES - 1
SCALE = DH ** (-0.5)
FAST = (6, 3, 3)
FULL = (8, 0, 0)

T_SEND, T_KEY, T_EXC, T_IN_Q, T_IN_K = 0, 56, 112, 120, 128
T_OUT, T_LOG, T_LIVE, T_BACK, T_BACK_LOG = 136, 168, 200, 232, 240
LOG_BACK, LOG_IN = 56, 112


def bf(x):
    return x.astype(jnp.bfloat16)


def attend(query, key, value_t, allowed=None):
    scores = lax.dot_general(
        key, query, (((1,), (1,)), ((), ())), preferred_element_type=jnp.float32
    ) * SCALE
    if allowed is not None:
        scores = jnp.where(allowed, scores, -1e30)
    top = jnp.max(scores, axis=0, keepdims=True)
    weights = jnp.exp(scores - top)
    total = jnp.sum(weights, axis=0, keepdims=True)
    out = jnp.dot(value_t, bf(weights), preferred_element_type=jnp.float32)
    return out / total, top + jnp.log(total)


def split_logs(logs, count):
    rows = list(logs) + [jnp.zeros_like(logs[0])] * (8 - count)
    whole = jnp.concatenate(rows, axis=0)
    high = bf(whole)
    low = bf(whole - high.astype(jnp.float32))
    return jnp.concatenate([high, low], axis=0)


def join_logs(tile):
    tile = tile.astype(jnp.float32)
    return tile[0:8] + tile[8:16]


def layer_kernel(
    cap, spare, back,
    table, q_hbm, k_hbm, v_hbm, w_hbm, o_ref, kv_far,
    q_own, q_all, kv_own, v_raw, q_out, q_in, o_in, o_all, exc_out, exc_in, back_out, back_in, in_plane, kv_buf,
    own_out, own_log, logs, att, wg, acc,
    load_sem, w_sem, qs_sem, qr_sem, os_sem, or_sem, es_sem, er_sem, bs_sem, br_sem, ks_sem, kr_sem, kl_sem,
    xs_sem, xr_sem,
):
    me = lax.axis_index("ctx")
    x = lax.axis_index("head")
    z = me // MATES
    y = (me % MATES) // 2
    core = me % 2
    msg = cap * BLK
    base_back = NZ * cap
    base_in = NZ * (cap + back)

    def at(dz, dy, dk, dx):
        ctx = ((z + dz) % PLANES) * MATES + ((y + dy) % 4) * 2 + (core + dk) % 2
        return (ctx, (x + dx) % HEADS)

    mates = [(dy, dk) for dy in range(4) for dk in range(2)][1:]

    def remote(src, dst, send, recv, device):
        return pltpu.make_async_remote_copy(
            src_ref=src, dst_ref=dst, send_sem=send, recv_sem=recv, device_id=device, device_id_type=MESH
        )

    def loads(h):
        cols = pl.ds(h * DH, DH)
        return [
            pltpu.make_async_copy(k_hbm.at[:, :, cols], kv_own.at[h, 0], load_sem.at[h, 0]),
            pltpu.make_async_copy(v_hbm.at[:, :, cols], v_raw.at[h], load_sem.at[h, 1]),
            pltpu.make_async_copy(q_hbm.at[:, :, cols], q_own.at[h], load_sem.at[h, 2]),
        ]

    for h in range(HEADS):
        for copy in loads(h):
            copy.start()
    own_w = pltpu.make_async_copy(
        w_hbm.at[:, pl.ds(pl.multiple_of(x * 512, 512), 512)], wg.at[0], w_sem.at[0, 0]
    )
    own_w.start()

    barrier = pltpu.get_barrier_semaphore()
    greet = [at(d, 0, 0, 0) for d in range(1, PLANES)]
    greet += [at(0, dy, dk, 0) for dy, dk in mates] + [at(0, 0, 0, d) for d in range(1, HEADS)]
    for device in greet:
        pl.semaphore_signal(barrier, inc=1, device_id=device, device_id_type=MESH)
    pl.semaphore_wait(barrier, len(greet))

    def w_copy(d):
        cols = pl.ds(pl.multiple_of(((x + d) % HEADS) * 512, 512), 512)
        return remote(w_hbm.at[:, cols], wg.at[HEADS - d], w_sem.at[0, d], w_sem.at[1, HEADS - d], at(0, 0, 0, d))

    def kv_near(h, dy):
        return remote(kv_own.at[h], kv_far.at[h, 2 * ((4 - dy) % 4)], ks_sem.at[h, dy], kr_sem.at[h, 2 * ((4 - dy) % 4)],
                      at(0, dy, 0, 0))

    def kv_next(h, part):
        dy, slot = (1, 6) if part == 0 else (3, 2)
        return remote(kv_far.at[h, slot, part], kv_far.at[h, 4, part], ks_sem.at[h, 4 + part],
                      kr_sem.at[h, 8 + part], at(0, dy, 0, 0))

    def kv_mate(h, dy):
        src = kv_own.at[h] if dy == 0 else kv_far.at[h, 2 * dy]
        return remote(src, kv_far.at[h, 2 * dy + 1], ks_sem.at[h, 6 + dy], kr_sem.at[h, 2 * dy + 1], at(0, 0, 1, 0))

    def exc_copy(h, n):
        dy, dk = mates[n]
        rel = ((4 - dy) % 4) * 2 + dk - 1
        return remote(exc_out.at[h], exc_in.at[h, rel], es_sem.at[h, n], er_sem.at[h, rel], at(0, dy, dk, 0))

    def q_copy(h, n):
        return remote(q_out.at[h, n], q_in.at[h, n, pl.ds(0, msg)], qs_sem.at[h, n], qr_sem.at[h, n], at(n + 1, 0, 0, 0))

    def o_copy(h, n):
        return remote(q_in.at[h, n], o_in.at[h, n], os_sem.at[h, n], or_sem.at[h, n], at(PLANES - 1 - n, 0, 0, 0))

    def back_copy(h, n):
        dy, dk = mates[n]
        rel = ((4 - dy) % 4) * 2 + dk - 1
        return remote(back_out.at[h], back_in.at[h, rel], bs_sem.at[h, n], br_sem.at[h, rel], at(0, dy, dk, 0))

    def x_copy(h, d):
        return remote(att.at[0, h], att.at[HEADS - d, h], xs_sem.at[h, d], xr_sem.at[h, HEADS - d], at(0, 0, 0, d))

    for h in range(HEADS):
        for copy in loads(h):
            copy.wait()

    @pl.loop(0, HEADS)
    def _(h):
        @pl.loop(0, BLOCKS)
        def _(b):
            kv_own[h, 1, b] = v_raw[h, b].T

        if spare:
            for e in range(spare):
                exc_out[h, e] = q_own[h, table[T_EXC + e]]
            for n in range(len(mates)):
                exc_copy(h, n).start()
        kv_near(h, 1).start()
        kv_near(h, 3).start()
        kv_mate(h, 0).start()

    for d in range(1, HEADS):
        w_copy(d).start()

    @pl.loop(0, HEADS)
    def _(h):
        if spare:
            for n in range(len(mates)):
                exc_copy(h, n).wait_recv()
            for n in range(len(mates)):
                for e in range(spare):
                    q_all[BLOCKS + n * spare + e] = exc_in[h, n, e]

        @pl.loop(0, BLOCKS)
        def _(b):
            q_all[b] = q_own[h, b]

        @pl.loop(0, NZ)
        def _(n):
            for i in range(cap):
                q_out[h, n, pl.ds(i * BLK, BLK), :] = q_all[table[T_SEND + n * 8 + i]]
            q_copy(h, n).start()

    def kv_first(h):
        for part, slot, dy in ((0, 6, 1), (1, 2, 3)):
            kv_near(h, dy).wait_recv()
            kv_next(h, part).start()
            kv_mate(h, 4 - dy).start()

    def kv_last(h):
        kv_next(h, 0).wait_recv()
        kv_next(h, 1).wait_recv()
        kv_mate(h, 2).start()
        own = pltpu.make_async_copy(kv_own.at[h], kv_buf.at[:, pl.ds(0, BLOCKS)], kl_sem.at[0])
        own.start()
        copies = [
            pltpu.make_async_copy(kv_far.at[h, n], kv_buf.at[:, pl.ds(n * BLOCKS, BLOCKS)], kl_sem.at[n])
            for n in range(1, MATES)
        ]
        for dy in (1, 2, 3):
            copies[2 * dy - 1].start()
        for dy in range(4):
            kv_mate(h, dy).wait_recv()
            copies[2 * dy].start()
        own.wait()
        for copy in copies:
            copy.wait()

    def kv_block(number):
        return kv_buf[0, number], kv_buf[1, number]

    def far_blocks(h):
        @pl.loop(0, NZ)
        def _(n):
            q_copy(h, n).wait_recv()
            outs, tops = [], []
            for i in range(cap):
                query = q_in[h, n, pl.ds(i * BLK, BLK), :]
                out, top = attend(query, *kv_block(table[T_KEY + n * 8 + i]))
                outs.append(bf(out))
                tops.append(top)
            for i in range(cap):
                q_in[h, n, pl.ds(i * BLK, BLK), :] = outs[i]
            q_in[h, n, pl.ds(msg, 16), :] = split_logs(tops, cap)
            o_copy(h, n).start()

        for j in range(MATES):
            out, top = attend(q_own[h, table[T_IN_Q + j]], *kv_block(table[T_IN_K + j]))
            in_plane[h % 2, j] = bf(out)
            logs[h, LOG_IN + j] = top

    def merge(h):
        causal = lax.broadcasted_iota(jnp.int32, (BLK, BLK), 0) <= lax.broadcasted_iota(jnp.int32, (BLK, BLK), 1)

        @pl.loop(0, BLOCKS // 2)
        def _(pair):
            for half in range(2):
                b = pair * 2 + half
                out, top = attend(q_own[h, b], kv_own[h, 0, b], kv_own[h, 1, b], causal)
                own_out[b] = out
                own_log[b] = top

        @pl.loop(0, MATES)
        def _(j):
            o_all[base_in + j] = in_plane[h % 2, j]

        @pl.loop(0, NZ)
        def _(n):
            o_copy(h, n).wait_recv()
            both = join_logs(o_in[h, n, pl.ds(msg, 16), :])
            for i in range(cap):
                o_all[n * cap + i] = o_in[h, n, pl.ds(i * BLK, BLK), :]
                logs[h, n * 8 + i] = both[i : i + 1]

        if back:
            tops = []
            for f in range(back):
                back_out[h, pl.ds(f * BLK, BLK), :] = o_all[table[T_BACK + f]]
                tops.append(logs[h, table[T_BACK_LOG + f]])
            back_out[h, pl.ds(back * BLK, 16), :] = split_logs(tops, back)
            for n in range(len(mates)):
                back_copy(h, n).start()
            for n in range(len(mates)):
                back_copy(h, n).wait_recv()
            for n in range(len(mates)):
                both = join_logs(back_in[h, n, pl.ds(back * BLK, 16), :])
                for f in range(back):
                    o_all[base_back + n * back + f] = back_in[h, n, pl.ds(f * BLK, BLK), :]
                    logs[h, LOG_BACK + n * 8 + f] = both[f : f + 1]

        @pl.loop(0, BLOCKS)
        def _(b):
            rows = pl.ds(pl.multiple_of(b * BLK, BLK), BLK)
            first = own_log[b]
            others, parts = [], []
            for j in range(2):
                item = b * 2 + j
                dead = (table[T_LIVE + item] - 1).astype(jnp.float32) * 1e30
                others.append(logs[h, table[T_LOG + item]] + dead)
                parts.append(o_all[table[T_OUT + item]].astype(jnp.float32))
            top = jnp.maximum(first, jnp.maximum(others[0], others[1]))
            weight = jnp.exp(first - top)
            total, merged = weight, weight * own_out[b]
            for other, part in zip(others, parts):
                weight = jnp.exp(other - top)
                total = total + weight
                merged = merged + weight * part
            att[0, h, rows, :] = bf(merged / total).T

        for d in range(1, HEADS):
            x_copy(h, d).start()

    def project(h):
        for d in range(1, HEADS):
            x_copy(h, d).wait_recv()
        weights = jnp.concatenate([wg[g, pl.ds(pl.multiple_of(h * DH, DH), DH), :] for g in range(HEADS)], axis=0)

        @pl.loop(0, ROWS // 256)
        def _(r):
            rows = pl.ds(pl.multiple_of(r * 256, 256), 256)
            left = jnp.concatenate([att[g, h, rows, :] for g in range(HEADS)], axis=1)
            acc[rows, :] = acc[rows, :] + jnp.dot(left, weights, preferred_element_type=jnp.float32)

    acc[...] = jnp.zeros_like(acc)
    own_w.wait()
    for d in range(1, HEADS):
        w_copy(d).wait_recv()
    kv_first(0)

    @pl.loop(0, HEADS + 2)
    def _(step):
        @pl.when(step + 1 < HEADS)
        def _():
            kv_first(step + 1)

        @pl.when(step < HEADS)
        def _():
            kv_last(step)
            far_blocks(step)

        @pl.when(jnp.logical_and(step >= 1, step <= HEADS))
        def _():
            merge(step - 1)

        @pl.when(step >= 2)
        def _():
            project(step - 2)

    @pl.loop(0, ROWS // 256)
    def _(r):
        rows = pl.ds(pl.multiple_of(r * 256, 256), 256)
        o_ref[rows, :] = bf(acc[rows, :])

    for d in range(1, HEADS):
        w_copy(d).wait_send()

    @pl.loop(0, HEADS)
    def _(h):
        kv_near(h, 1).wait_send()
        kv_near(h, 3).wait_send()
        for part in range(2):
            kv_next(h, part).wait_send()
        for dy in range(4):
            kv_mate(h, dy).wait_send()
        for n in range(NZ):
            q_copy(h, n).wait_send()
            o_copy(h, n).wait_send()
        for n in range(len(mates)):
            if spare:
                exc_copy(h, n).wait_send()
            if back:
                back_copy(h, n).wait_send()
        for d in range(1, HEADS):
            x_copy(h, d).wait_send()


def layer(sizes, number, table, queries, keys, values, out_weight):
    cap, spare, back = sizes
    msg = cap * BLK
    tile = (BLK, DH)
    b16 = jnp.bfloat16
    dma = pltpu.SemaphoreType.DMA
    any_space = pl.BlockSpec(memory_space=pl.ANY)
    out, _ = pl.pallas_call(
        functools.partial(layer_kernel, cap, spare, back),
        name=f"layer_{cap}",
        out_shape=(
            jax.ShapeDtypeStruct((ROWS, 512), b16),
            jax.ShapeDtypeStruct((HEADS, MATES, 2, BLOCKS) + tile, b16),
        ),
        in_specs=[pl.BlockSpec(memory_space=pltpu.SMEM)] + [any_space] * 4,
        out_specs=(pl.BlockSpec(memory_space=pltpu.VMEM), any_space),
        scratch_shapes=[
            pltpu.VMEM((HEADS, BLOCKS) + tile, b16),
            pltpu.VMEM((BLOCKS + NZ * spare,) + tile, b16),
            pltpu.VMEM((HEADS, 2, BLOCKS) + tile, b16),
            pltpu.VMEM((HEADS, BLOCKS) + tile, b16),
            pltpu.VMEM((HEADS, NZ, msg, DH), b16),
            pltpu.VMEM((HEADS, NZ, msg + 16, DH), b16),
            pltpu.VMEM((HEADS, NZ, msg + 16, DH), b16),
            pltpu.VMEM((NZ * (cap + back) + MATES,) + tile, b16),
            pltpu.VMEM((HEADS, max(spare, 1)) + tile, b16),
            pltpu.VMEM((HEADS, NZ, max(spare, 1)) + tile, b16),
            pltpu.VMEM((HEADS, back * BLK + 16, DH), b16),
            pltpu.VMEM((HEADS, NZ, back * BLK + 16, DH), b16),
            pltpu.VMEM((2, MATES) + tile, b16),
            pltpu.VMEM((2, MATES * BLOCKS) + tile, b16),
            pltpu.VMEM((BLOCKS,) + tile, jnp.float32),
            pltpu.VMEM((BLOCKS, 1, DH), jnp.float32),
            pltpu.VMEM((HEADS, 120, 1, DH), jnp.float32),
            pltpu.VMEM((HEADS, HEADS, ROWS, DH), b16),
            pltpu.VMEM((HEADS, 512, 512), b16),
            pltpu.VMEM((ROWS, 512), jnp.float32),
            dma((HEADS, 3)), dma((2, HEADS)),
            dma((HEADS, NZ)), dma((HEADS, NZ)), dma((HEADS, NZ)), dma((HEADS, NZ)),
            dma((HEADS, NZ)), dma((HEADS, NZ)), dma((HEADS, NZ)), dma((HEADS, NZ)),
            dma((HEADS, 10)), dma((HEADS, 10)), dma((MATES,)),
            dma((HEADS, HEADS)), dma((HEADS, HEADS)),
        ],
        compiler_params=pltpu.CompilerParams(
            collective_id=number, has_side_effects=True, vmem_limit_bytes=63 << 20
        ),
    )(table, *[array.reshape(BLOCKS, BLK, -1) for array in (queries, keys, values)], out_weight)
    return out


def total(mask, value, axes):
    return jnp.sum(jnp.where(mask, value, 0), axis=axes)


def route(places, cap, spare, back):
    eight = jnp.arange(8, dtype=jnp.int32)
    item = jnp.arange(32, dtype=jnp.int32)
    plane = jnp.where(places >= 0, places // 128, -1)
    source = eight[:, None, None]
    goes = plane[..., None] == eight
    away = (plane >= 0) & (plane != source)
    count = jnp.sum(goes, axis=2, dtype=jnp.int32)
    earlier = item[None, :] < item[:, None]
    rank = jnp.sum((plane[..., None, :] == plane[..., :, None]) & earlier, axis=-1, dtype=jnp.int32)
    over = away & (rank >= cap)
    spare_rank = jnp.sum(over[..., None, :] & earlier, axis=-1, dtype=jnp.int32)
    apart = eight[:, None, None] != eight
    over_count = jnp.where(apart, jnp.maximum(count - cap, 0), 0)
    room = jnp.where(apart, jnp.maximum(cap - count, 0), 0)
    before = eight[None, :] < eight[:, None]
    over_before = total(before[None, :, :, None], over_count[:, None], 2)
    order = (eight[:, None] - eight[None, :]) % 8
    first = order[None, :, :] < order[:, None, :]
    room_before = total(first[None], room[:, None], 2)
    turn = total(goes, over_before[:, :, None, :], -1) + rank - cap
    mine = goes[:, :, :, None, :]
    low = total(mine, room_before[:, None, None], -1)
    size = total(mine, room[:, None, None], -1)
    filled = total(mine, count[:, None, None], -1)
    turn8 = turn[..., None]
    hit = over[..., None] & (low <= turn8) & (turn8 < low + size)
    carrier = jnp.where(over, total(hit, eight, -1), eight[None, :, None])
    slot = jnp.where(over, total(hit, filled + turn8 - low, -1), rank)
    flat_over, flat_carrier = over.reshape(8, 256), jnp.where(over, carrier, -1).reshape(8, 256)
    flat = jnp.arange(256, dtype=jnp.int32)
    same = flat_over[:, None, :] & (flat_carrier[:, None, :] == flat_carrier[:, :, None])
    back_rank = jnp.sum(same & (flat[None, :] < flat[:, None]), axis=-1, dtype=jnp.int32).reshape(8, 8, 32)
    fits = ~over | (jnp.any(hit, axis=-1) & (spare_rank < spare) & (back_rank < back))
    return plane, rank, over, spare_rank, carrier, slot, back_rank, jnp.all(fits)


def make_table(places, routed, me, cap, spare, back):
    plane, rank, over, spare_rank, carrier, slot, back_rank, _ = routed
    eight = jnp.arange(8, dtype=jnp.int32)
    item = jnp.arange(32, dtype=jnp.int32)
    z, w = me // 8, me % 8

    def relative(device):
        return ((device // 2 - w // 2) % 4) * 2 + (device - w) % 2

    def here(array):
        return lax.dynamic_index_in_dim(array, z, 0, keepdims=False)

    def own(array):
        return lax.dynamic_index_in_dim(here(array), w, 0, keepdims=False)

    shift = jnp.arange(7, dtype=jnp.int32)[:, None, None, None]
    step = (plane - z) % 8 - 1
    key = relative((places % 128) // 16) * 16 + places % 16

    plane_h, over_h, spare_h, carrier_h, slot_h, back_h, step_h = map(
        here, (plane, over, spare_rank, carrier, slot, back_rank, step)
    )
    sent = (plane_h >= 0) & (plane_h != z) & (carrier_h == w)
    source = jnp.where(
        eight[:, None] == w, item[None, :] // 2, 16 + (relative(eight)[:, None] - 1) * spare + spare_h
    )
    slots = eight[None, :, None, None]
    send = total(sent & (step_h == shift) & (slot_h == slots), source, (-1, -2))
    comes = (plane == z) & (eight[:, None, None] != z) & (carrier == w)
    from_step = ((z - eight) % 8 - 1)[:, None, None]
    arrive = total(comes & (from_step == shift[..., None]) & (slot == slots[..., None]), key, (-1, -2, -3))

    plane_o, over_o, spare_o, carrier_o, slot_o, back_o, step_o, rank_o, key_o = map(
        own, (plane, over, spare_rank, carrier, slot, back_rank, step, rank, key)
    )
    exc = total(over_o & (spare_o == eight[:, None]), item // 2, -1)
    inside = plane_o == z
    local = inside & (rank_o == eight[:, None])
    in_q = total(local, item // 2, -1)
    in_k = total(local, key_o, -1)
    rel = relative(carrier_o) - 1
    place = jnp.where(over_o, 7 * cap + rel * back + back_o, step_o * cap + slot_o)
    place = jnp.where(inside, 7 * (cap + back) + rank_o, place)
    log = jnp.where(over_o, LOG_BACK + rel * 8 + back_o, step_o * 8 + slot_o)
    log = jnp.where(inside, LOG_IN + rank_o, log)
    live = plane_o >= 0
    place, log = jnp.where(live, place, 0), jnp.where(live, log, 0)
    foreign = over_h & (carrier_h == w) & (back_h == eight[:, None, None])
    back_place = total(foreign, step_h * cap + slot_h, (-1, -2))
    back_log = total(foreign, step_h * 8 + slot_h, (-1, -2))
    pieces = [send.reshape(-1), arrive.reshape(-1), exc, in_q, in_k, place, log, live, back_place, back_log]
    return jnp.concatenate([piece.astype(jnp.int32) for piece in pieces])


def shards(queries, keys, values, out_weight, block_order, selection):
    me = lax.axis_index("ctx")
    stored = jnp.arange(block_order.shape[0], dtype=jnp.int32)
    wanted = selection.reshape(-1)
    own_ids = lax.dynamic_slice_in_dim(block_order, me * BLOCKS, BLOCKS)
    where_stored = total(wanted[:, None] == block_order[None, :], stored[None, :], -1)
    mine = jnp.where(wanted != jnp.repeat(own_ids, 2), where_stored, -1)
    places = lax.all_gather(mine, "ctx").reshape(8, 8, 32)
    arrays = (queries, keys, values, out_weight)
    routed = route(places, *FAST)

    def fast():
        return layer(FAST, 0, make_table(places, routed, me, *FAST), *arrays)

    def full():
        return layer(FULL, 1, make_table(places, route(places, *FULL), me, *FULL), *arrays)

    return lax.cond(routed[-1], fast, full)


def solution(mesh):
    return jax.shard_map(
        shards,
        mesh=mesh,
        in_specs=(
            P("ctx", "head"),
            P("ctx", "head"),
            P("ctx", "head"),
            P("head", None),
            P(),
            P("ctx", None),
        ),
        out_specs=P("ctx", "head"),
        check_vma=False,
    )
```

```python
import functools

import jax
import jax.numpy as jnp
from jax import lax
from jax.experimental import pallas as pl
from jax.experimental.pallas import tpu as pltpu
from jax.sharding import PartitionSpec as P

MESH = pl.DeviceIdType.MESH
DH = 128
BLK = 128
HEADS = 4
BLOCKS = 16
ROWS = BLOCKS * BLK
PLANES = 8
MATES = 8
NZ = PLANES - 1
SCALE = DH ** (-0.5)
SIZES = ((5, 0, 4, 5), (5, 1, 4, 5), (8, 0, 0, 0))

T_SEND, T_KEY, T_EXC, T_IN_Q, T_IN_K = 0, 56, 112, 120, 128
T_OUT, T_LOG, T_LIVE, T_BACK, T_BACK_LOG = 136, 168, 200, 232, 240
LOG_BACK, LOG_IN = 56, 112


def bf(x):
    return x.astype(jnp.bfloat16)


def attend(query, key, value_t, allowed=None):
    scores = lax.dot_general(
        key, query, (((1,), (1,)), ((), ())), preferred_element_type=jnp.float32
    ) * SCALE
    if allowed is not None:
        scores = jnp.where(allowed, scores, -1e30)
    top = jnp.max(scores, axis=0, keepdims=True)
    weights = jnp.exp(scores - top)
    total = jnp.sum(weights, axis=0, keepdims=True)
    out = jnp.dot(value_t, bf(weights), preferred_element_type=jnp.float32)
    return out / total, top + jnp.log(total)


def split_logs(logs, count):
    rows = list(logs) + [jnp.zeros_like(logs[0])] * (8 - count)
    whole = jnp.concatenate(rows, axis=0)
    high = bf(whole)
    low = bf(whole - high.astype(jnp.float32))
    return jnp.concatenate([high, low], axis=0)


def join_logs(tile):
    tile = tile.astype(jnp.float32)
    return tile[0:8] + tile[8:16]


def layer_kernel(
    cap, extra, spare, back,
    table, q_hbm, k_hbm, v_hbm, w_hbm, o_ref, kv_far,
    q_own, q_all, kv_own, q_out, q_in, o_in, qx_out, qx_in, ox_in, o_all, exc_out, exc_in, back_out, back_in, in_plane, kv_buf,
    own_out, own_log, logs, att, wg, acc,
    load_sem, w_sem, qs_sem, qr_sem, os_sem, or_sem, qxs_sem, qxr_sem, oxs_sem, oxr_sem, es_sem, er_sem, bs_sem, br_sem, ks_sem, kr_sem, kl_sem,
    xs_sem, xr_sem,
):
    me = lax.axis_index("ctx")
    x = lax.axis_index("head")
    z = me // MATES
    y = (me % MATES) // 2
    core = me % 2
    msg = cap * BLK
    base_extra = NZ * cap
    base_back = base_extra + 4 * extra
    base_in = base_back + NZ * back

    def more(n):
        return (n + core) % 2 == 0

    def at(dz, dy, dk, dx):
        ctx = ((z + dz) % PLANES) * MATES + ((y + dy) % 4) * 2 + (core + dk) % 2
        return (ctx, (x + dx) % HEADS)

    mates = [(dy, dk) for dy in range(4) for dk in range(2)][1:]

    def remote(src, dst, send, recv, device):
        return pltpu.make_async_remote_copy(
            src_ref=src, dst_ref=dst, send_sem=send, recv_sem=recv, device_id=device, device_id_type=MESH
        )

    def load(h, part):
        src = (q_hbm, k_hbm, v_hbm)[part].at[:, :, pl.ds(h * DH, DH)]
        return pltpu.make_async_copy(src, q_own.at[h] if part == 0 else kv_own.at[h, part - 1], load_sem.at[h, part])

    for part in range(3):
        for h in range(HEADS):
            load(h, part).start()
    own_w = pltpu.make_async_copy(
        w_hbm.at[:, pl.ds(pl.multiple_of(x * 512, 512), 512)], wg.at[0], w_sem.at[0, 0]
    )
    own_w.start()

    barrier = pltpu.get_barrier_semaphore()
    greet = [at(d, 0, 0, 0) for d in range(1, PLANES)]
    greet += [at(0, dy, dk, 0) for dy, dk in mates] + [at(0, 0, 0, d) for d in range(1, HEADS)]
    for device in greet:
        pl.semaphore_signal(barrier, inc=1, device_id=device, device_id_type=MESH)
    pl.semaphore_wait(barrier, len(greet))

    def w_copy(d):
        cols = pl.ds(pl.multiple_of(((x + d) % HEADS) * 512, 512), 512)
        return remote(w_hbm.at[:, cols], wg.at[HEADS - d], w_sem.at[0, d], w_sem.at[1, HEADS - d], at(0, 0, 0, d))

    def kv_near(h, dy):
        return remote(kv_own.at[h], kv_far.at[h, 2 * ((4 - dy) % 4)], ks_sem.at[h, dy], kr_sem.at[h, 2 * ((4 - dy) % 4)],
                      at(0, dy, 0, 0))

    def kv_next(h, part):
        dy, slot = (1, 6) if part == 0 else (3, 2)
        return remote(kv_far.at[h, slot, part], kv_far.at[h, 4, part], ks_sem.at[h, 4 + part],
                      kr_sem.at[h, 8 + part], at(0, dy, 0, 0))

    def kv_mate(h, dy):
        src = kv_own.at[h] if dy == 0 else kv_far.at[h, 2 * dy]
        return remote(src, kv_far.at[h, 2 * dy + 1], ks_sem.at[h, 6 + dy], kr_sem.at[h, 2 * dy + 1], at(0, 0, 1, 0))

    def near(out, into, send, recv, h, dy):
        slot = 2 * ((4 - dy) % 4) - 1
        return remote(out.at[h], into.at[h, slot], send.at[h, dy], recv.at[h, slot], at(0, dy, 0, 0))

    def mate(out, into, send, recv, h, dy):
        src = out.at[h] if dy == 0 else into.at[h, 2 * dy - 1]
        return remote(src, into.at[h, 2 * dy], send.at[h, 4 + dy], recv.at[h, 2 * dy], at(0, 0, 1, 0))

    def spread_start(arrays, h):
        mate(*arrays, h, 0).start()
        for dy in range(1, 4):
            near(*arrays, h, dy).start()

    def spread_finish(arrays, h):
        for dy in range(1, 4):
            near(*arrays, h, 4 - dy).wait_recv()
            mate(*arrays, h, dy).start()
        for dy in range(4):
            mate(*arrays, h, dy).wait_recv()

    def spread_drain(arrays, h):
        for dy in range(4):
            mate(*arrays, h, dy).wait_send()
        for dy in range(1, 4):
            near(*arrays, h, dy).wait_send()

    exc = (exc_out, exc_in, es_sem, er_sem)
    handed = (back_out, back_in, bs_sem, br_sem)

    def qx_copy(h, n):
        return remote(qx_out.at[h, n // 2], qx_in.at[h, n // 2, pl.ds(0, BLK)], qxs_sem.at[h, n // 2],
                      qxr_sem.at[h, n // 2], at(n + 1, 0, 0, 0))

    def ox_copy(h, n):
        return remote(qx_in.at[h, n // 2], ox_in.at[h, n // 2], oxs_sem.at[h, n // 2], oxr_sem.at[h, n // 2],
                      at(PLANES - 1 - n, 0, 0, 0))

    def q_copy(h, n):
        return remote(q_out.at[h, n], q_in.at[h, n, pl.ds(0, msg)], qs_sem.at[h, n], qr_sem.at[h, n], at(n + 1, 0, 0, 0))

    def o_copy(h, n):
        return remote(q_in.at[h, n], o_in.at[h, n], os_sem.at[h, n], or_sem.at[h, n], at(PLANES - 1 - n, 0, 0, 0))

    def x_copy(h, d):
        return remote(att.at[0, h], att.at[HEADS - d, h], xs_sem.at[h, d], xr_sem.at[h, HEADS - d], at(0, 0, 0, d))

    for h in range(HEADS):
        load(h, 0).wait()
    if spare:
        @pl.loop(0, HEADS)
        def _(h):
            for e in range(spare):
                exc_out[h, e] = q_own[h, table[T_EXC + e]]
            spread_start(exc, h)

    for h in range(HEADS):
        for part in (1, 2):
            load(h, part).wait()

    @pl.loop(0, HEADS)
    def _(h):
        @pl.loop(0, BLOCKS)
        def _(b):
            kv_own[h, 1, b] = kv_own[h, 1, b].T
            q_all[b] = q_own[h, b]

        kv_near(h, 1).start()
        kv_near(h, 3).start()
        kv_mate(h, 0).start()

        if spare:
            spread_finish(exc, h)
            for n in range(NZ):
                for e in range(spare):
                    q_all[BLOCKS + n * spare + e] = exc_in[h, n, e]

        @pl.loop(0, NZ)
        def _(n):
            for i in range(cap):
                q_out[h, n, pl.ds(i * BLK, BLK), :] = q_all[table[T_SEND + n * 8 + i]]
            q_copy(h, n).start()
            if extra:
                @pl.when(more(n))
                def _():
                    qx_out[h, n // 2] = q_all[table[T_SEND + n * 8 + cap]]
                    qx_copy(h, n).start()

    for d in range(1, HEADS):
        w_copy(d).start()

    def kv_first(h):
        for part, slot, dy in ((0, 6, 1), (1, 2, 3)):
            kv_near(h, dy).wait_recv()
            kv_next(h, part).start()
            kv_mate(h, 4 - dy).start()

    def kv_last(h):
        kv_next(h, 0).wait_recv()
        kv_next(h, 1).wait_recv()
        kv_mate(h, 2).start()
        own = pltpu.make_async_copy(kv_own.at[h], kv_buf.at[:, pl.ds(0, BLOCKS)], kl_sem.at[0])
        own.start()
        copies = [
            pltpu.make_async_copy(kv_far.at[h, n], kv_buf.at[:, pl.ds(n * BLOCKS, BLOCKS)], kl_sem.at[n])
            for n in range(1, MATES)
        ]
        for dy in (1, 2, 3):
            copies[2 * dy - 1].start()
        for dy in range(4):
            kv_mate(h, dy).wait_recv()
            copies[2 * dy].start()
        own.wait()
        for copy in copies:
            copy.wait()

    def kv_block(number):
        return kv_buf[0, number], kv_buf[1, number]

    def far_blocks(h):
        @pl.loop(0, NZ)
        def _(n):
            q_copy(h, n).wait_recv()
            outs, tops = [], []
            for i in range(cap):
                query = q_in[h, n, pl.ds(i * BLK, BLK), :]
                out, top = attend(query, *kv_block(table[T_KEY + n * 8 + i]))
                outs.append(bf(out))
                tops.append(top)
            for i in range(cap):
                q_in[h, n, pl.ds(i * BLK, BLK), :] = outs[i]
            q_in[h, n, pl.ds(msg, 16), :] = split_logs(tops, cap)
            o_copy(h, n).start()
            if extra:
                @pl.when(more(n))
                def _():
                    qx_copy(h, n).wait_recv()
                    query = qx_in[h, n // 2, pl.ds(0, BLK), :]
                    out, top = attend(query, *kv_block(table[T_KEY + n * 8 + cap]))
                    qx_in[h, n // 2, pl.ds(0, BLK), :] = bf(out)
                    qx_in[h, n // 2, pl.ds(BLK, 16), :] = split_logs([top], 1)
                    ox_copy(h, n).start()

        for j in range(MATES):
            out, top = attend(q_own[h, table[T_IN_Q + j]], *kv_block(table[T_IN_K + j]))
            in_plane[h % 2, j] = bf(out)
            logs[h, LOG_IN + j] = top

    def merge(h):
        causal = lax.broadcasted_iota(jnp.int32, (BLK, BLK), 0) <= lax.broadcasted_iota(jnp.int32, (BLK, BLK), 1)

        @pl.loop(0, BLOCKS // 2)
        def _(pair):
            for half in range(2):
                b = pair * 2 + half
                out, top = attend(q_own[h, b], kv_own[h, 0, b], kv_own[h, 1, b], causal)
                own_out[b] = out
                own_log[b] = top

        @pl.loop(0, MATES)
        def _(j):
            o_all[base_in + j] = in_plane[h % 2, j]

        @pl.loop(0, NZ)
        def _(n):
            o_copy(h, n).wait_recv()
            both = join_logs(o_in[h, n, pl.ds(msg, 16), :])
            for i in range(cap):
                o_all[n * cap + i] = o_in[h, n, pl.ds(i * BLK, BLK), :]
                logs[h, n * 8 + i] = both[i : i + 1]
            if extra:
                @pl.when(more(n))
                def _():
                    ox_copy(h, n).wait_recv()
                    o_all[base_extra + n // 2] = ox_in[h, n // 2, pl.ds(0, BLK), :]
                    logs[h, n * 8 + cap] = join_logs(ox_in[h, n // 2, pl.ds(BLK, 16), :])[0:1]

        if back:
            tops = []
            for f in range(back):
                back_out[h, pl.ds(f * BLK, BLK), :] = o_all[table[T_BACK + f]]
                tops.append(logs[h, table[T_BACK_LOG + f]])
            back_out[h, pl.ds(back * BLK, 16), :] = split_logs(tops, back)
            spread_start(handed, h)
            spread_finish(handed, h)
            for n in range(NZ):
                both = join_logs(back_in[h, n, pl.ds(back * BLK, 16), :])
                for f in range(back):
                    o_all[base_back + n * back + f] = back_in[h, n, pl.ds(f * BLK, BLK), :]
                    logs[h, LOG_BACK + n * 8 + f] = both[f : f + 1]

        @pl.loop(0, BLOCKS)
        def _(b):
            rows = pl.ds(pl.multiple_of(b * BLK, BLK), BLK)
            first = own_log[b]
            others, parts = [], []
            for j in range(2):
                item = b * 2 + j
                dead = (table[T_LIVE + item] - 1).astype(jnp.float32) * 1e30
                others.append(logs[h, table[T_LOG + item]] + dead)
                parts.append(o_all[table[T_OUT + item]].astype(jnp.float32))
            top = jnp.maximum(first, jnp.maximum(others[0], others[1]))
            weight = jnp.exp(first - top)
            total, merged = weight, weight * own_out[b]
            for other, part in zip(others, parts):
                weight = jnp.exp(other - top)
                total = total + weight
                merged = merged + weight * part
            att[0, h, rows, :] = bf(merged / total).T

        for d in range(1, HEADS):
            x_copy(h, d).start()

    def project(h):
        for d in range(1, HEADS):
            x_copy(h, d).wait_recv()
        weights = jnp.concatenate([wg[g, pl.ds(pl.multiple_of(h * DH, DH), DH), :] for g in range(HEADS)], axis=0)

        @pl.loop(0, ROWS // 256)
        def _(r):
            rows = pl.ds(pl.multiple_of(r * 256, 256), 256)
            left = jnp.concatenate([att[g, h, rows, :] for g in range(HEADS)], axis=1)
            acc[rows, :] = acc[rows, :] + jnp.dot(left, weights, preferred_element_type=jnp.float32)

    acc[...] = jnp.zeros_like(acc)
    own_w.wait()
    for d in range(1, HEADS):
        w_copy(d).wait_recv()
    kv_first(0)

    @pl.loop(0, HEADS + 2)
    def _(step):
        @pl.when(step + 1 < HEADS)
        def _():
            kv_first(step + 1)

        @pl.when(step < HEADS)
        def _():
            kv_last(step)
            far_blocks(step)

        @pl.when(jnp.logical_and(step >= 1, step <= HEADS))
        def _():
            merge(step - 1)

        @pl.when(step >= 2)
        def _():
            project(step - 2)

    @pl.loop(0, ROWS // 256)
    def _(r):
        rows = pl.ds(pl.multiple_of(r * 256, 256), 256)
        o_ref[rows, :] = bf(acc[rows, :])

    for d in range(1, HEADS):
        w_copy(d).wait_send()

    @pl.loop(0, HEADS)
    def _(h):
        kv_near(h, 1).wait_send()
        kv_near(h, 3).wait_send()
        for part in range(2):
            kv_next(h, part).wait_send()
        for dy in range(4):
            kv_mate(h, dy).wait_send()
        for n in range(NZ):
            q_copy(h, n).wait_send()
            o_copy(h, n).wait_send()
            if extra:
                @pl.when(more(n))
                def _():
                    qx_copy(h, n).wait_send()
                    ox_copy(h, n).wait_send()
        if spare:
            spread_drain(exc, h)
        if back:
            spread_drain(handed, h)
        for d in range(1, HEADS):
            x_copy(h, d).wait_send()


def layer(sizes, number, table, queries, keys, values, out_weight):
    cap, extra, spare, back = sizes
    msg = cap * BLK
    tile = (BLK, DH)
    few = 4 if extra else 1
    b16 = jnp.bfloat16
    dma = pltpu.SemaphoreType.DMA
    any_space = pl.BlockSpec(memory_space=pl.ANY)
    out, _ = pl.pallas_call(
        functools.partial(layer_kernel, cap, extra, spare, back),
        name=f"layer_{cap}_{extra}",
        out_shape=(
            jax.ShapeDtypeStruct((ROWS, 512), b16),
            jax.ShapeDtypeStruct((HEADS, MATES, 2, BLOCKS) + tile, b16),
        ),
        in_specs=[pl.BlockSpec(memory_space=pltpu.SMEM)] + [any_space] * 4,
        out_specs=(pl.BlockSpec(memory_space=pltpu.VMEM), any_space),
        scratch_shapes=[
            pltpu.VMEM((HEADS, BLOCKS) + tile, b16),
            pltpu.VMEM((BLOCKS + NZ * spare,) + tile, b16),
            pltpu.VMEM((HEADS, 2, BLOCKS) + tile, b16),
            pltpu.VMEM((HEADS, NZ, msg, DH), b16),
            pltpu.VMEM((HEADS, NZ, msg + 16, DH), b16),
            pltpu.VMEM((HEADS, NZ, msg + 16, DH), b16),
            pltpu.VMEM((HEADS, few, BLK, DH), b16),
            pltpu.VMEM((HEADS, few, BLK + 16, DH), b16),
            pltpu.VMEM((HEADS, few, BLK + 16, DH), b16),
            pltpu.VMEM((NZ * (cap + back) + 4 * extra + MATES,) + tile, b16),
            pltpu.VMEM((HEADS, max(spare, 1)) + tile, b16),
            pltpu.VMEM((HEADS, NZ, max(spare, 1)) + tile, b16),
            pltpu.VMEM((HEADS, back * BLK + 16, DH), b16),
            pltpu.VMEM((HEADS, NZ, back * BLK + 16, DH), b16),
            pltpu.VMEM((2, MATES) + tile, b16),
            pltpu.VMEM((2, MATES * BLOCKS) + tile, b16),
            pltpu.VMEM((BLOCKS,) + tile, jnp.float32),
            pltpu.VMEM((BLOCKS, 1, DH), jnp.float32),
            pltpu.VMEM((HEADS, 120, 1, DH), jnp.float32),
            pltpu.VMEM((HEADS, HEADS, ROWS, DH), b16),
            pltpu.VMEM((HEADS, 512, 512), b16),
            pltpu.VMEM((ROWS, 512), jnp.float32),
            dma((HEADS, 3)), dma((2, HEADS)),
            dma((HEADS, NZ)), dma((HEADS, NZ)), dma((HEADS, NZ)), dma((HEADS, NZ)),
            dma((HEADS, 4)), dma((HEADS, 4)), dma((HEADS, 4)), dma((HEADS, 4)),
            dma((HEADS, 8)), dma((HEADS, NZ)), dma((HEADS, 8)), dma((HEADS, NZ)),
            dma((HEADS, 10)), dma((HEADS, 10)), dma((MATES,)),
            dma((HEADS, HEADS)), dma((HEADS, HEADS)),
        ],
        compiler_params=pltpu.CompilerParams(
            collective_id=number, has_side_effects=True, vmem_limit_bytes=63 << 20
        ),
    )(table, *[array.reshape(BLOCKS, BLK, -1) for array in (queries, keys, values)], out_weight)
    return out


def swap_kernel(mine, out, every, send_sem, recv_sem):
    me = lax.axis_index("ctx")
    x = lax.axis_index("head")
    z, w = me // MATES, me % MATES
    planes = [((z + d) % PLANES * MATES + w, x) for d in range(1, PLANES)]
    mates = [(z * MATES + (w + d) % MATES, x) for d in range(1, MATES)]
    barrier = pltpu.get_barrier_semaphore()
    for device in planes + mates:
        pl.semaphore_signal(barrier, inc=1, device_id=device, device_id_type=MESH)
    pl.semaphore_wait(barrier, len(planes + mates))
    every[w, z] = mine[...]
    for stage, devices, part in ((0, planes, every.at[w, z]), (1, mates, every.at[w])):
        copies = [
            pltpu.make_async_remote_copy(
                src_ref=part, dst_ref=part, send_sem=send_sem.at[stage, n], recv_sem=recv_sem.at[stage, n],
                device_id=device, device_id_type=MESH,
            )
            for n, device in enumerate(devices)
        ]
        for copy in copies:
            copy.start()
        for copy in copies:
            copy.wait()
    out[...] = every[...]


def swap(mine):
    vmem = pl.BlockSpec(memory_space=pltpu.VMEM)
    shape = (MATES, PLANES, 1, DH)
    return pl.pallas_call(
        swap_kernel,
        name="swap",
        out_shape=jax.ShapeDtypeStruct(shape, jnp.int32),
        in_specs=[vmem],
        out_specs=vmem,
        scratch_shapes=[
            pltpu.VMEM(shape, jnp.int32), pltpu.SemaphoreType.DMA((2, 7)), pltpu.SemaphoreType.DMA((2, 7))
        ],
        compiler_params=pltpu.CompilerParams(collective_id=3, has_side_effects=True),
    )(mine)


def total(mask, value, axes):
    return jnp.sum(jnp.where(mask, value, 0), axis=axes)


def room_of(cap, extra):
    eight = jnp.arange(8, dtype=jnp.int32)
    step = (eight - eight[:, None, None]) % 8 - 1
    more = (step + eight[None, :, None]) % 2 == 0
    return jnp.where(more, cap + extra, cap)


def route(places, cap, extra, spare, back):
    eight = jnp.arange(8, dtype=jnp.int32)
    item = jnp.arange(32, dtype=jnp.int32)
    plane = jnp.where(places >= 0, places // 128, -1)
    source = eight[:, None, None]
    goes = plane[..., None] == eight
    away = (plane >= 0) & (plane != source)
    count = jnp.sum(goes, axis=2, dtype=jnp.int32)
    earlier = item[None, :] < item[:, None]
    rank = jnp.sum((plane[..., None, :] == plane[..., :, None]) & earlier, axis=-1, dtype=jnp.int32)
    limit = room_of(cap, extra)
    own_limit = total(goes, limit[:, :, None, :], -1)
    over = away & (rank >= own_limit)
    spare_rank = jnp.sum(over[..., None, :] & earlier, axis=-1, dtype=jnp.int32)
    apart = eight[:, None, None] != eight
    over_count = jnp.where(apart, jnp.maximum(count - limit, 0), 0)
    room = jnp.where(apart, jnp.maximum(limit - count, 0), 0)
    before = eight[None, :] < eight[:, None]
    over_before = total(before[None, :, :, None], over_count[:, None], 2)
    order = (eight[:, None] - eight[None, :]) % 8
    first = order[None, :, :] < order[:, None, :]
    room_before = total(first[None], room[:, None], 2)
    turn = total(goes, over_before[:, :, None, :], -1) + rank - own_limit
    mine = goes[:, :, :, None, :]
    low = total(mine, room_before[:, None, None], -1)
    size = total(mine, room[:, None, None], -1)
    filled = total(mine, count[:, None, None], -1)
    turn8 = turn[..., None]
    hit = over[..., None] & (low <= turn8) & (turn8 < low + size)
    carrier = jnp.where(over, total(hit, eight, -1), eight[None, :, None])
    slot = jnp.where(over, total(hit, filled + turn8 - low, -1), rank)
    flat_over, flat_carrier = over.reshape(8, 256), jnp.where(over, carrier, -1).reshape(8, 256)
    flat = jnp.arange(256, dtype=jnp.int32)
    same = flat_over[:, None, :] & (flat_carrier[:, None, :] == flat_carrier[:, :, None])
    back_rank = jnp.sum(same & (flat[None, :] < flat[:, None]), axis=-1, dtype=jnp.int32).reshape(8, 8, 32)
    fits = ~over | (jnp.any(hit, axis=-1) & (spare_rank < spare) & (back_rank < back))
    return plane, rank, over, spare_rank, carrier, slot, back_rank, jnp.all(fits)


def make_table(places, routed, me, cap, extra, spare, back):
    plane, rank, over, spare_rank, carrier, slot, back_rank, _ = routed
    eight = jnp.arange(8, dtype=jnp.int32)
    item = jnp.arange(32, dtype=jnp.int32)
    z, w = me // 8, me % 8

    def relative(device):
        return ((device // 2 - w // 2) % 4) * 2 + (device - w) % 2

    def here(array):
        return lax.dynamic_index_in_dim(array, z, 0, keepdims=False)

    def own(array):
        return lax.dynamic_index_in_dim(here(array), w, 0, keepdims=False)

    shift = jnp.arange(7, dtype=jnp.int32)[:, None, None, None]
    step = (plane - z) % 8 - 1
    key = relative((places % 128) // 16) * 16 + places % 16

    plane_h, over_h, spare_h, carrier_h, slot_h, back_h, step_h = map(
        here, (plane, over, spare_rank, carrier, slot, back_rank, step)
    )
    sent = (plane_h >= 0) & (plane_h != z) & (carrier_h == w)
    source = jnp.where(
        eight[:, None] == w, item[None, :] // 2, 16 + (relative(eight)[:, None] - 1) * spare + spare_h
    )
    slots = eight[None, :, None, None]
    send = total(sent & (step_h == shift) & (slot_h == slots), source, (-1, -2))
    comes = (plane == z) & (eight[:, None, None] != z) & (carrier == w)
    from_step = ((z - eight) % 8 - 1)[:, None, None]
    arrive = total(comes & (from_step == shift[..., None]) & (slot == slots[..., None]), key, (-1, -2, -3))

    plane_o, over_o, spare_o, carrier_o, slot_o, back_o, step_o, rank_o, key_o = map(
        own, (plane, over, spare_rank, carrier, slot, back_rank, step, rank, key)
    )
    exc = total(over_o & (spare_o == eight[:, None]), item // 2, -1)
    inside = plane_o == z
    local = inside & (rank_o == eight[:, None])
    in_q = total(local, item // 2, -1)
    in_k = total(local, key_o, -1)
    rel = relative(carrier_o) - 1
    def far_place(step, slot):
        return jnp.where(slot == cap, 7 * cap + step // 2, step * cap + slot)

    base_back = 7 * cap + 4 * extra
    place = jnp.where(over_o, base_back + rel * back + back_o, far_place(step_o, slot_o))
    place = jnp.where(inside, base_back + 7 * back + rank_o, place)
    log = jnp.where(over_o, LOG_BACK + rel * 8 + back_o, step_o * 8 + slot_o)
    log = jnp.where(inside, LOG_IN + rank_o, log)
    live = plane_o >= 0
    place, log = jnp.where(live, place, 0), jnp.where(live, log, 0)
    foreign = over_h & (carrier_h == w) & (back_h == eight[:, None, None])
    back_place = total(foreign, far_place(step_h, slot_h), (-1, -2))
    back_log = total(foreign, step_h * 8 + slot_h, (-1, -2))
    pieces = [send.reshape(-1), arrive.reshape(-1), exc, in_q, in_k, place, log, live, back_place, back_log]
    return jnp.concatenate([piece.astype(jnp.int32) for piece in pieces])


def shards(queries, keys, values, out_weight, block_order, selection):
    me = lax.axis_index("ctx")
    stored = jnp.arange(block_order.shape[0], dtype=jnp.int32)
    wanted = selection.reshape(-1)
    own_ids = lax.dynamic_slice_in_dim(block_order, me * BLOCKS, BLOCKS)
    where_stored = total(wanted[:, None] == block_order[None, :], stored[None, :], -1)
    mine = jnp.where(wanted != jnp.repeat(own_ids, 2), where_stored, -1)
    every = swap(jnp.pad(mine, (0, DH - mine.shape[0])).reshape(1, DH))
    places = jnp.swapaxes(every[:, :, 0, :32], 0, 1)
    arrays = (queries, keys, values, out_weight)
    eight = jnp.arange(8, dtype=jnp.int32)
    count = jnp.sum((places // 128)[..., None] == eight, axis=2, dtype=jnp.int32)
    count = jnp.where(eight[:, None, None] != eight, count, 0)
    many = jnp.sum(count, axis=1) > 8 * SIZES[0][0]
    over = jnp.sum(jnp.maximum(count - SIZES[0][0], 0), axis=2) > SIZES[0][2]
    extra = (jnp.any(many) | jnp.any(over)).astype(jnp.int32)
    routed = route(places, SIZES[0][0], extra, *SIZES[0][2:])

    def variant(number):
        def run():
            sizes = SIZES[number]
            used = route(places, *sizes) if number == 2 else routed
            return layer(sizes, number, make_table(places, used, me, *sizes), *arrays)

        return run

    return lax.switch(jnp.where(routed[-1], extra, 2), [variant(number) for number in range(3)])


def solution(mesh):
    return jax.shard_map(
        shards,
        mesh=mesh,
        in_specs=(
            P("ctx", "head"),
            P("ctx", "head"),
            P("ctx", "head"),
            P("head", None),
            P(),
            P("ctx", None),
        ),
        out_specs=P("ctx", "head"),
        check_vma=False,
    )
```

```python
import functools

import jax
import jax.numpy as jnp
from jax import lax
from jax.experimental import pallas as pl
from jax.experimental.pallas import tpu as pltpu
from jax.sharding import PartitionSpec as P

MESH = pl.DeviceIdType.MESH
DH = 128
BLK = 128
HEADS = 4
BLOCKS = 16
ROWS = BLOCKS * BLK
PLANES = 8
MATES = 8
NZ = PLANES - 1
SCALE = DH ** (-0.5)
SIZES = ((5, 0, 4, 5), (5, 1, 4, 5), (8, 0, 0, 0))

T_SEND, T_KEY, T_EXC, T_IN_Q, T_IN_K = 0, 56, 112, 120, 128
T_OUT, T_LOG, T_LIVE, T_BACK, T_BACK_LOG = 136, 168, 200, 232, 240
LOG_BACK, LOG_IN = 56, 112


def bf(x):
    return x.astype(jnp.bfloat16)


def attend(query, key, value_t, allowed=None):
    scores = lax.dot_general(
        key, query, (((1,), (1,)), ((), ())), preferred_element_type=jnp.float32
    ) * SCALE
    if allowed is not None:
        scores = jnp.where(allowed, scores, -1e30)
    top = jnp.max(scores, axis=0, keepdims=True)
    weights = jnp.exp(scores - top)
    total = jnp.sum(weights, axis=0, keepdims=True)
    out = jnp.dot(value_t, bf(weights), preferred_element_type=jnp.float32)
    return out / total, top + jnp.log(total)


def split_logs(logs, count):
    rows = list(logs) + [jnp.zeros_like(logs[0])] * (8 - count)
    whole = jnp.concatenate(rows, axis=0)
    high = bf(whole)
    low = bf(whole - high.astype(jnp.float32))
    return jnp.concatenate([high, low], axis=0)


def join_logs(tile):
    tile = tile.astype(jnp.float32)
    return tile[0:8] + tile[8:16]


def layer_kernel(
    cap, extra, spare, back,
    table, q_hbm, k_hbm, v_hbm, w_hbm, o_ref, kv_far,
    q_own, q_all, kv_own, q_out, q_in, o_in, qx_out, qx_in, ox_in, o_all, exc_out, exc_in, back_out, back_in, in_plane, kv_buf,
    own_out, own_log, logs, att, wg, acc,
    load_sem, w_sem, qs_sem, qr_sem, os_sem, or_sem, qxs_sem, qxr_sem, oxs_sem, oxr_sem, es_sem, er_sem, bs_sem, br_sem, ks_sem, kr_sem, kl_sem,
    xs_sem, xr_sem,
):
    me = lax.axis_index("ctx")
    x = lax.axis_index("head")
    z = me // MATES
    y = (me % MATES) // 2
    core = me % 2
    msg = cap * BLK
    base_extra = NZ * cap
    base_back = base_extra + 4 * extra
    base_in = base_back + NZ * back

    def more(n):
        return (n + core) % 2 == 0

    def at(dz, dy, dk, dx):
        ctx = ((z + dz) % PLANES) * MATES + ((y + dy) % 4) * 2 + (core + dk) % 2
        return (ctx, (x + dx) % HEADS)

    mates = [(dy, dk) for dy in range(4) for dk in range(2)][1:]

    def remote(src, dst, send, recv, device):
        return pltpu.make_async_remote_copy(
            src_ref=src, dst_ref=dst, send_sem=send, recv_sem=recv, device_id=device, device_id_type=MESH
        )

    def load(h, part):
        src = (q_hbm, k_hbm, v_hbm)[part].at[:, :, pl.ds(h * DH, DH)]
        return pltpu.make_async_copy(src, q_own.at[h] if part == 0 else kv_own.at[h, part - 1], load_sem.at[h, part])

    for part in range(3):
        for h in range(HEADS):
            load(h, part).start()
    own_w = pltpu.make_async_copy(
        w_hbm.at[:, pl.ds(pl.multiple_of(x * 512, 512), 512)], wg.at[0], w_sem.at[0, 0]
    )
    own_w.start()

    barrier = pltpu.get_barrier_semaphore()
    greet = [at(d, 0, 0, 0) for d in range(1, PLANES)]
    greet += [at(0, dy, dk, 0) for dy, dk in mates] + [at(0, 0, 0, d) for d in range(1, HEADS)]
    for device in greet:
        pl.semaphore_signal(barrier, inc=1, device_id=device, device_id_type=MESH)
    pl.semaphore_wait(barrier, len(greet))

    def w_copy(d):
        cols = pl.ds(pl.multiple_of(((x + d) % HEADS) * 512, 512), 512)
        return remote(w_hbm.at[:, cols], wg.at[HEADS - d], w_sem.at[0, d], w_sem.at[1, HEADS - d], at(0, 0, 0, d))

    def kv_near(h, dy):
        return remote(kv_own.at[h], kv_far.at[h, 2 * ((4 - dy) % 4)], ks_sem.at[h, dy], kr_sem.at[h, 2 * ((4 - dy) % 4)],
                      at(0, dy, 0, 0))

    def kv_next(h, part):
        dy, slot = (1, 6) if part == 0 else (3, 2)
        return remote(kv_far.at[h, slot, part], kv_far.at[h, 4, part], ks_sem.at[h, 4 + part],
                      kr_sem.at[h, 8 + part], at(0, dy, 0, 0))

    def kv_mate(h, dy):
        src = kv_own.at[h] if dy == 0 else kv_far.at[h, 2 * dy]
        return remote(src, kv_far.at[h, 2 * dy + 1], ks_sem.at[h, 6 + dy], kr_sem.at[h, 2 * dy + 1], at(0, 0, 1, 0))

    def near(out, into, send, recv, h, dy):
        slot = 2 * ((4 - dy) % 4) - 1
        return remote(out.at[h], into.at[h, slot], send.at[h, dy], recv.at[h, slot], at(0, dy, 0, 0))

    def mate(out, into, send, recv, h, dy):
        src = out.at[h] if dy == 0 else into.at[h, 2 * dy - 1]
        return remote(src, into.at[h, 2 * dy], send.at[h, 4 + dy], recv.at[h, 2 * dy], at(0, 0, 1, 0))

    def spread_start(arrays, h):
        mate(*arrays, h, 0).start()
        for dy in range(1, 4):
            near(*arrays, h, dy).start()

    def spread_finish(arrays, h):
        for dy in range(1, 4):
            near(*arrays, h, 4 - dy).wait_recv()
            mate(*arrays, h, dy).start()
        for dy in range(4):
            mate(*arrays, h, dy).wait_recv()

    def spread_drain(arrays, h):
        for dy in range(4):
            mate(*arrays, h, dy).wait_send()
        for dy in range(1, 4):
            near(*arrays, h, dy).wait_send()

    exc = (exc_out, exc_in, es_sem, er_sem)
    handed = (back_out, back_in, bs_sem, br_sem)

    def qx_copy(h, n):
        return remote(qx_out.at[h, n // 2], qx_in.at[h, n // 2, pl.ds(0, BLK)], qxs_sem.at[h, n // 2],
                      qxr_sem.at[h, n // 2], at(n + 1, 0, 0, 0))

    def ox_copy(h, n):
        return remote(qx_in.at[h, n // 2], ox_in.at[h, n // 2], oxs_sem.at[h, n // 2], oxr_sem.at[h, n // 2],
                      at(PLANES - 1 - n, 0, 0, 0))

    def q_copy(h, n):
        return remote(q_out.at[h, n], q_in.at[h, n, pl.ds(0, msg)], qs_sem.at[h, n], qr_sem.at[h, n], at(n + 1, 0, 0, 0))

    def o_copy(h, n):
        return remote(q_in.at[h, n], o_in.at[h, n], os_sem.at[h, n], or_sem.at[h, n], at(PLANES - 1 - n, 0, 0, 0))

    def x_copy(h, d):
        return remote(att.at[0, h], att.at[HEADS - d, h], xs_sem.at[h, d], xr_sem.at[h, HEADS - d], at(0, 0, 0, d))

    for h in range(HEADS):
        load(h, 0).wait()
    def spare_start(h):
        if spare:
            for e in range(spare):
                exc_out[h, e] = q_own[h, table[T_EXC + e]]
            spread_start(exc, h)

    def kv_start(h):
        @pl.loop(0, BLOCKS)
        def _(b):
            kv_own[h, 1, b] = kv_own[h, 1, b].T

        kv_near(h, 1).start()
        kv_near(h, 3).start()
        kv_mate(h, 0).start()

    def send_queries(h):
        @pl.loop(0, BLOCKS)
        def _(b):
            q_all[b] = q_own[h, b]

        if spare:
            spread_finish(exc, h)
            for n in range(NZ):
                for e in range(spare):
                    q_all[BLOCKS + n * spare + e] = exc_in[h, n, e]

        @pl.loop(0, NZ)
        def _(n):
            for i in range(cap):
                q_out[h, n, pl.ds(i * BLK, BLK), :] = q_all[table[T_SEND + n * 8 + i]]
            q_copy(h, n).start()
            if extra:
                @pl.when(more(n))
                def _():
                    qx_out[h, n // 2] = q_all[table[T_SEND + n * 8 + cap]]
                    qx_copy(h, n).start()

    spare_start(0)
    spare_start(1)
    for h in range(HEADS):
        for part in (1, 2):
            load(h, part).wait()
    kv_start(0)

    @pl.loop(0, 2)
    def _(h):
        send_queries(h)
        spare_start(h + 2)

    for d in range(1, HEADS):
        w_copy(d).start()

    def kv_first(h):
        for part, dy in ((0, 1), (1, 3)):
            kv_near(h, dy).wait_recv()
            kv_next(h, part).start()
            kv_mate(h, 4 - dy).start()

        @pl.when(h + 1 < HEADS)
        def _():
            kv_start(h + 1)

    def kv_last(h):
        kv_next(h, 0).wait_recv()
        kv_next(h, 1).wait_recv()
        kv_mate(h, 2).start()
        own = pltpu.make_async_copy(kv_own.at[h], kv_buf.at[:, pl.ds(0, BLOCKS)], kl_sem.at[0])
        own.start()
        copies = [
            pltpu.make_async_copy(kv_far.at[h, n], kv_buf.at[:, pl.ds(n * BLOCKS, BLOCKS)], kl_sem.at[n])
            for n in range(1, MATES)
        ]
        for dy in (1, 2, 3):
            copies[2 * dy - 1].start()
        for dy in range(4):
            kv_mate(h, dy).wait_recv()
            copies[2 * dy].start()
        own.wait()
        for copy in copies:
            copy.wait()

    def kv_block(number):
        return kv_buf[0, number], kv_buf[1, number]

    def far_blocks(h):
        @pl.loop(0, NZ)
        def _(n):
            q_copy(h, n).wait_recv()
            outs, tops = [], []
            for i in range(cap):
                query = q_in[h, n, pl.ds(i * BLK, BLK), :]
                out, top = attend(query, *kv_block(table[T_KEY + n * 8 + i]))
                outs.append(bf(out))
                tops.append(top)
            for i in range(cap):
                q_in[h, n, pl.ds(i * BLK, BLK), :] = outs[i]
            q_in[h, n, pl.ds(msg, 16), :] = split_logs(tops, cap)
            o_copy(h, n).start()
            if extra:
                @pl.when(more(n))
                def _():
                    qx_copy(h, n).wait_recv()
                    query = qx_in[h, n // 2, pl.ds(0, BLK), :]
                    out, top = attend(query, *kv_block(table[T_KEY + n * 8 + cap]))
                    qx_in[h, n // 2, pl.ds(0, BLK), :] = bf(out)
                    qx_in[h, n // 2, pl.ds(BLK, 16), :] = split_logs([top], 1)
                    ox_copy(h, n).start()

        for j in range(MATES):
            out, top = attend(q_own[h, table[T_IN_Q + j]], *kv_block(table[T_IN_K + j]))
            in_plane[h, j] = bf(out)
            logs[h, LOG_IN + j] = top

    def own_blocks(h):
        causal = lax.broadcasted_iota(jnp.int32, (BLK, BLK), 0) <= lax.broadcasted_iota(jnp.int32, (BLK, BLK), 1)

        @pl.loop(0, BLOCKS // 2)
        def _(pair):
            for half in range(2):
                b = pair * 2 + half
                out, top = attend(q_own[h, b], kv_own[h, 0, b], kv_own[h, 1, b], causal)
                own_out[b] = out
                own_log[b] = top

    def merge(h):
        @pl.loop(0, MATES)
        def _(j):
            o_all[base_in + j] = in_plane[h, j]

        @pl.loop(0, NZ)
        def _(n):
            o_copy(h, n).wait_recv()
            both = join_logs(o_in[h, n, pl.ds(msg, 16), :])
            for i in range(cap):
                o_all[n * cap + i] = o_in[h, n, pl.ds(i * BLK, BLK), :]
                logs[h, n * 8 + i] = both[i : i + 1]
            if extra:
                @pl.when(more(n))
                def _():
                    ox_copy(h, n).wait_recv()
                    o_all[base_extra + n // 2] = ox_in[h, n // 2, pl.ds(0, BLK), :]
                    logs[h, n * 8 + cap] = join_logs(ox_in[h, n // 2, pl.ds(BLK, 16), :])[0:1]

        if back:
            tops = []
            for f in range(back):
                back_out[h, pl.ds(f * BLK, BLK), :] = o_all[table[T_BACK + f]]
                tops.append(logs[h, table[T_BACK_LOG + f]])
            back_out[h, pl.ds(back * BLK, 16), :] = split_logs(tops, back)
            spread_start(handed, h)
            own_blocks(h)
            spread_finish(handed, h)
            for n in range(NZ):
                both = join_logs(back_in[h, n, pl.ds(back * BLK, 16), :])
                for f in range(back):
                    o_all[base_back + n * back + f] = back_in[h, n, pl.ds(f * BLK, BLK), :]
                    logs[h, LOG_BACK + n * 8 + f] = both[f : f + 1]
        else:
            own_blocks(h)

        @pl.loop(0, BLOCKS)
        def _(b):
            rows = pl.ds(pl.multiple_of(b * BLK, BLK), BLK)
            first = own_log[b]
            others, parts = [], []
            for j in range(2):
                item = b * 2 + j
                dead = (table[T_LIVE + item] - 1).astype(jnp.float32) * 1e30
                others.append(logs[h, table[T_LOG + item]] + dead)
                parts.append(o_all[table[T_OUT + item]].astype(jnp.float32))
            top = jnp.maximum(first, jnp.maximum(others[0], others[1]))
            weight = jnp.exp(first - top)
            total, merged = weight, weight * own_out[b]
            for other, part in zip(others, parts):
                weight = jnp.exp(other - top)
                total = total + weight
                merged = merged + weight * part
            att[0, h, rows, :] = bf(merged / total).T

        for d in range(1, HEADS):
            x_copy(h, d).start()

    def project(h):
        for d in range(1, HEADS):
            x_copy(h, d).wait_recv()
        weights = jnp.concatenate([wg[g, pl.ds(pl.multiple_of(h * DH, DH), DH), :] for g in range(HEADS)], axis=0)

        @pl.loop(0, ROWS // 256)
        def _(r):
            rows = pl.ds(pl.multiple_of(r * 256, 256), 256)
            left = jnp.concatenate([att[g, h, rows, :] for g in range(HEADS)], axis=1)
            acc[rows, :] = acc[rows, :] + jnp.dot(left, weights, preferred_element_type=jnp.float32)

    kv_first(0)

    @pl.loop(0, HEADS)
    def _(h):
        kv_last(h)

        @pl.when(h < 2)
        def _():
            send_queries(h + 2)

        far_blocks(h)

        @pl.when(h + 1 < HEADS)
        def _():
            kv_first(h + 1)

        @pl.when(h >= 1)
        def _():
            merge(h - 1)

    acc[...] = jnp.zeros_like(acc)
    own_w.wait()
    for d in range(1, HEADS):
        w_copy(d).wait_recv()

    project(0)
    project(1)
    merge(HEADS - 1)
    project(2)
    project(3)

    @pl.loop(0, ROWS // 256)
    def _(r):
        rows = pl.ds(pl.multiple_of(r * 256, 256), 256)
        o_ref[rows, :] = bf(acc[rows, :])

    for d in range(1, HEADS):
        w_copy(d).wait_send()

    @pl.loop(0, HEADS)
    def _(h):
        kv_near(h, 1).wait_send()
        kv_near(h, 3).wait_send()
        for part in range(2):
            kv_next(h, part).wait_send()
        for dy in range(4):
            kv_mate(h, dy).wait_send()
        for n in range(NZ):
            q_copy(h, n).wait_send()
            o_copy(h, n).wait_send()
            if extra:
                @pl.when(more(n))
                def _():
                    qx_copy(h, n).wait_send()
                    ox_copy(h, n).wait_send()
        if spare:
            spread_drain(exc, h)
        if back:
            spread_drain(handed, h)
        for d in range(1, HEADS):
            x_copy(h, d).wait_send()


def layer(sizes, number, table, queries, keys, values, out_weight):
    cap, extra, spare, back = sizes
    msg = cap * BLK
    tile = (BLK, DH)
    few = 4 if extra else 1
    b16 = jnp.bfloat16
    dma = pltpu.SemaphoreType.DMA
    any_space = pl.BlockSpec(memory_space=pl.ANY)
    out, _ = pl.pallas_call(
        functools.partial(layer_kernel, cap, extra, spare, back),
        name=f"layer_{cap}_{extra}",
        out_shape=(
            jax.ShapeDtypeStruct((ROWS, 512), b16),
            jax.ShapeDtypeStruct((HEADS, MATES, 2, BLOCKS) + tile, b16),
        ),
        in_specs=[pl.BlockSpec(memory_space=pltpu.SMEM)] + [any_space] * 4,
        out_specs=(pl.BlockSpec(memory_space=pltpu.VMEM), any_space),
        scratch_shapes=[
            pltpu.VMEM((HEADS, BLOCKS) + tile, b16),
            pltpu.VMEM((BLOCKS + NZ * spare,) + tile, b16),
            pltpu.VMEM((HEADS, 2, BLOCKS) + tile, b16),
            pltpu.VMEM((HEADS, NZ, msg, DH), b16),
            pltpu.VMEM((HEADS, NZ, msg + 16, DH), b16),
            pltpu.VMEM((HEADS, NZ, msg + 16, DH), b16),
            pltpu.VMEM((HEADS, few, BLK, DH), b16),
            pltpu.VMEM((HEADS, few, BLK + 16, DH), b16),
            pltpu.VMEM((HEADS, few, BLK + 16, DH), b16),
            pltpu.VMEM((NZ * (cap + back) + 4 * extra + MATES,) + tile, b16),
            pltpu.VMEM((HEADS, max(spare, 1)) + tile, b16),
            pltpu.VMEM((HEADS, NZ, max(spare, 1)) + tile, b16),
            pltpu.VMEM((HEADS, back * BLK + 16, DH), b16),
            pltpu.VMEM((HEADS, NZ, back * BLK + 16, DH), b16),
            pltpu.VMEM((HEADS, MATES) + tile, b16),
            pltpu.VMEM((2, MATES * BLOCKS) + tile, b16),
            pltpu.VMEM((BLOCKS,) + tile, jnp.float32),
            pltpu.VMEM((BLOCKS, 1, DH), jnp.float32),
            pltpu.VMEM((HEADS, 120, 1, DH), jnp.float32),
            pltpu.VMEM((HEADS, HEADS, ROWS, DH), b16),
            pltpu.VMEM((HEADS, 512, 512), b16),
            pltpu.VMEM((ROWS, 512), jnp.float32),
            dma((HEADS, 3)), dma((2, HEADS)),
            dma((HEADS, NZ)), dma((HEADS, NZ)), dma((HEADS, NZ)), dma((HEADS, NZ)),
            dma((HEADS, 4)), dma((HEADS, 4)), dma((HEADS, 4)), dma((HEADS, 4)),
            dma((HEADS, 8)), dma((HEADS, NZ)), dma((HEADS, 8)), dma((HEADS, NZ)),
            dma((HEADS, 10)), dma((HEADS, 10)), dma((MATES,)),
            dma((HEADS, HEADS)), dma((HEADS, HEADS)),
        ],
        compiler_params=pltpu.CompilerParams(
            collective_id=number, has_side_effects=True, vmem_limit_bytes=63 << 20
        ),
    )(table, *[array.reshape(BLOCKS, BLK, -1) for array in (queries, keys, values)], out_weight)
    return out


def swap_kernel(mine, out, every, send_sem, recv_sem):
    me = lax.axis_index("ctx")
    x = lax.axis_index("head")
    z, w = me // MATES, me % MATES
    planes = [((z + d) % PLANES * MATES + w, x) for d in range(1, PLANES)]
    mates = [(z * MATES + (w + d) % MATES, x) for d in range(1, MATES)]
    barrier = pltpu.get_barrier_semaphore()
    for device in planes + mates:
        pl.semaphore_signal(barrier, inc=1, device_id=device, device_id_type=MESH)
    pl.semaphore_wait(barrier, len(planes + mates))
    every[w, z] = mine[...]
    for stage, devices, part in ((0, planes, every.at[w, z]), (1, mates, every.at[w])):
        copies = [
            pltpu.make_async_remote_copy(
                src_ref=part, dst_ref=part, send_sem=send_sem.at[stage, n], recv_sem=recv_sem.at[stage, n],
                device_id=device, device_id_type=MESH,
            )
            for n, device in enumerate(devices)
        ]
        for copy in copies:
            copy.start()
        for copy in copies:
            copy.wait()
    out[...] = every[...]


def swap(mine):
    vmem = pl.BlockSpec(memory_space=pltpu.VMEM)
    shape = (MATES, PLANES, 1, DH)
    return pl.pallas_call(
        swap_kernel,
        name="swap",
        out_shape=jax.ShapeDtypeStruct(shape, jnp.int32),
        in_specs=[vmem],
        out_specs=vmem,
        scratch_shapes=[
            pltpu.VMEM(shape, jnp.int32), pltpu.SemaphoreType.DMA((2, 7)), pltpu.SemaphoreType.DMA((2, 7))
        ],
        compiler_params=pltpu.CompilerParams(collective_id=3, has_side_effects=True),
    )(mine)


def total(mask, value, axes):
    return jnp.sum(jnp.where(mask, value, 0), axis=axes)


def room_of(cap, extra):
    eight = jnp.arange(8, dtype=jnp.int32)
    step = (eight - eight[:, None, None]) % 8 - 1
    more = (step + eight[None, :, None]) % 2 == 0
    return jnp.where(more, cap + extra, cap)


def route(places, cap, extra, spare, back):
    eight = jnp.arange(8, dtype=jnp.int32)
    item = jnp.arange(32, dtype=jnp.int32)
    plane = jnp.where(places >= 0, places // 128, -1)
    source = eight[:, None, None]
    goes = plane[..., None] == eight
    away = (plane >= 0) & (plane != source)
    count = jnp.sum(goes, axis=2, dtype=jnp.int32)
    earlier = item[None, :] < item[:, None]
    rank = jnp.sum((plane[..., None, :] == plane[..., :, None]) & earlier, axis=-1, dtype=jnp.int32)
    limit = room_of(cap, extra)
    own_limit = total(goes, limit[:, :, None, :], -1)
    over = away & (rank >= own_limit)
    spare_rank = jnp.sum(over[..., None, :] & earlier, axis=-1, dtype=jnp.int32)
    apart = eight[:, None, None] != eight
    over_count = jnp.where(apart, jnp.maximum(count - limit, 0), 0)
    room = jnp.where(apart, jnp.maximum(limit - count, 0), 0)
    before = eight[None, :] < eight[:, None]
    over_before = total(before[None, :, :, None], over_count[:, None], 2)
    order = (eight[:, None] - eight[None, :]) % 8
    first = order[None, :, :] < order[:, None, :]
    room_before = total(first[None], room[:, None], 2)
    turn = total(goes, over_before[:, :, None, :], -1) + rank - own_limit
    mine = goes[:, :, :, None, :]
    low = total(mine, room_before[:, None, None], -1)
    size = total(mine, room[:, None, None], -1)
    filled = total(mine, count[:, None, None], -1)
    turn8 = turn[..., None]
    hit = over[..., None] & (low <= turn8) & (turn8 < low + size)
    carrier = jnp.where(over, total(hit, eight, -1), eight[None, :, None])
    slot = jnp.where(over, total(hit, filled + turn8 - low, -1), rank)
    flat_over, flat_carrier = over.reshape(8, 256), jnp.where(over, carrier, -1).reshape(8, 256)
    flat = jnp.arange(256, dtype=jnp.int32)
    same = flat_over[:, None, :] & (flat_carrier[:, None, :] == flat_carrier[:, :, None])
    back_rank = jnp.sum(same & (flat[None, :] < flat[:, None]), axis=-1, dtype=jnp.int32).reshape(8, 8, 32)
    fits = ~over | (jnp.any(hit, axis=-1) & (spare_rank < spare) & (back_rank < back))
    return plane, rank, over, spare_rank, carrier, slot, back_rank, jnp.all(fits)


def make_table(places, routed, me, cap, extra, spare, back):
    plane, rank, over, spare_rank, carrier, slot, back_rank, _ = routed
    eight = jnp.arange(8, dtype=jnp.int32)
    item = jnp.arange(32, dtype=jnp.int32)
    z, w = me // 8, me % 8

    def relative(device):
        return ((device // 2 - w // 2) % 4) * 2 + (device - w) % 2

    def here(array):
        return lax.dynamic_index_in_dim(array, z, 0, keepdims=False)

    def own(array):
        return lax.dynamic_index_in_dim(here(array), w, 0, keepdims=False)

    shift = jnp.arange(7, dtype=jnp.int32)[:, None, None, None]
    step = (plane - z) % 8 - 1
    key = relative((places % 128) // 16) * 16 + places % 16

    plane_h, over_h, spare_h, carrier_h, slot_h, back_h, step_h = map(
        here, (plane, over, spare_rank, carrier, slot, back_rank, step)
    )
    sent = (plane_h >= 0) & (plane_h != z) & (carrier_h == w)
    source = jnp.where(
        eight[:, None] == w, item[None, :] // 2, 16 + (relative(eight)[:, None] - 1) * spare + spare_h
    )
    slots = eight[None, :, None, None]
    send = total(sent & (step_h == shift) & (slot_h == slots), source, (-1, -2))
    comes = (plane == z) & (eight[:, None, None] != z) & (carrier == w)
    from_step = ((z - eight) % 8 - 1)[:, None, None]
    arrive = total(comes & (from_step == shift[..., None]) & (slot == slots[..., None]), key, (-1, -2, -3))

    plane_o, over_o, spare_o, carrier_o, slot_o, back_o, step_o, rank_o, key_o = map(
        own, (plane, over, spare_rank, carrier, slot, back_rank, step, rank, key)
    )
    exc = total(over_o & (spare_o == eight[:, None]), item // 2, -1)
    inside = plane_o == z
    local = inside & (rank_o == eight[:, None])
    in_q = total(local, item // 2, -1)
    in_k = total(local, key_o, -1)
    rel = relative(carrier_o) - 1
    def far_place(step, slot):
        return jnp.where(slot == cap, 7 * cap + step // 2, step * cap + slot)

    base_back = 7 * cap + 4 * extra
    place = jnp.where(over_o, base_back + rel * back + back_o, far_place(step_o, slot_o))
    place = jnp.where(inside, base_back + 7 * back + rank_o, place)
    log = jnp.where(over_o, LOG_BACK + rel * 8 + back_o, step_o * 8 + slot_o)
    log = jnp.where(inside, LOG_IN + rank_o, log)
    live = plane_o >= 0
    place, log = jnp.where(live, place, 0), jnp.where(live, log, 0)
    foreign = over_h & (carrier_h == w) & (back_h == eight[:, None, None])
    back_place = total(foreign, far_place(step_h, slot_h), (-1, -2))
    back_log = total(foreign, step_h * 8 + slot_h, (-1, -2))
    pieces = [send.reshape(-1), arrive.reshape(-1), exc, in_q, in_k, place, log, live, back_place, back_log]
    return jnp.concatenate([piece.astype(jnp.int32) for piece in pieces])


def shards(queries, keys, values, out_weight, block_order, selection):
    me = lax.axis_index("ctx")
    stored = jnp.arange(block_order.shape[0], dtype=jnp.int32)
    wanted = selection.reshape(-1)
    own_ids = lax.dynamic_slice_in_dim(block_order, me * BLOCKS, BLOCKS)
    where_stored = total(wanted[:, None] == block_order[None, :], stored[None, :], -1)
    mine = jnp.where(wanted != jnp.repeat(own_ids, 2), where_stored, -1)
    every = swap(jnp.pad(mine, (0, DH - mine.shape[0])).reshape(1, DH))
    places = jnp.swapaxes(every[:, :, 0, :32], 0, 1)
    arrays = (queries, keys, values, out_weight)
    eight = jnp.arange(8, dtype=jnp.int32)
    count = jnp.sum((places // 128)[..., None] == eight, axis=2, dtype=jnp.int32)
    count = jnp.where(eight[:, None, None] != eight, count, 0)
    many = jnp.sum(count, axis=1) > 8 * SIZES[0][0]
    over = jnp.sum(jnp.maximum(count - SIZES[0][0], 0), axis=2) > SIZES[0][2]
    extra = (jnp.any(many) | jnp.any(over)).astype(jnp.int32)
    routed = route(places, SIZES[0][0], extra, *SIZES[0][2:])

    def variant(number):
        def run():
            sizes = SIZES[number]
            used = route(places, *sizes) if number == 2 else routed
            return layer(sizes, number, make_table(places, used, me, *sizes), *arrays)

        return run

    return lax.switch(jnp.where(routed[-1], extra, 2), [variant(number) for number in range(3)])


def solution(mesh):
    return jax.shard_map(
        shards,
        mesh=mesh,
        in_specs=(
            P("ctx", "head"),
            P("ctx", "head"),
            P("ctx", "head"),
            P("head", None),
            P(),
            P("ctx", None),
        ),
        out_specs=P("ctx", "head"),
        check_vma=False,
    )
```

```python
import functools

import jax
import jax.numpy as jnp
from jax import lax
from jax.experimental import pallas as pl
from jax.experimental.pallas import tpu as pltpu
from jax.sharding import PartitionSpec as P

MESH = pl.DeviceIdType.MESH
DH = 128
BLK = 128
HEADS = 4
BLOCKS = 16
ROWS = BLOCKS * BLK
PLANES = 8
MATES = 8
NZ = PLANES - 1
SCALE = DH ** (-0.5)
SIZES = ((5, 0, 4, 5), (5, 1, 4, 5), (8, 0, 0, 0))

T_SEND, T_KEY, T_EXC, T_IN_Q, T_IN_K = 0, 56, 112, 120, 128
T_OUT, T_LOG, T_LIVE, T_BACK, T_BACK_LOG = 136, 168, 200, 232, 240
LOG_BACK, LOG_IN = 56, 112


def bf(x):
    return x.astype(jnp.bfloat16)


def attend(query, key, value_t, allowed=None):
    scores = lax.dot_general(
        key, query, (((1,), (1,)), ((), ())), preferred_element_type=jnp.float32
    ) * SCALE
    if allowed is not None:
        scores = jnp.where(allowed, scores, -1e30)
    top = jnp.max(scores, axis=0, keepdims=True)
    weights = jnp.exp(scores - top)
    total = jnp.sum(weights, axis=0, keepdims=True)
    out = jnp.dot(value_t, bf(weights), preferred_element_type=jnp.float32)
    return out / total, top + jnp.log(total)


def split_logs(logs, count):
    rows = list(logs) + [jnp.zeros_like(logs[0])] * (8 - count)
    whole = jnp.concatenate(rows, axis=0)
    high = bf(whole)
    low = bf(whole - high.astype(jnp.float32))
    return jnp.concatenate([high, low], axis=0)


def join_logs(tile):
    tile = tile.astype(jnp.float32)
    return tile[0:8] + tile[8:16]


def layer_kernel(
    cap, extra, spare, back,
    table, q_hbm, k_hbm, v_hbm, w_hbm, o_ref, kv_far,
    q_own, q_all, kv_own, q_out, q_in, o_in, qx_out, qx_in, ox_in, o_all, exc_out, exc_in, back_out, back_in, in_plane, kv_buf,
    own_out, own_log, logs, att, wg, acc,
    load_sem, w_sem, qs_sem, qr_sem, os_sem, or_sem, qxs_sem, qxr_sem, oxs_sem, oxr_sem, es_sem, er_sem, bs_sem, br_sem, ks_sem, kr_sem, kl_sem,
    xs_sem, xr_sem,
):
    me = lax.axis_index("ctx")
    x = lax.axis_index("head")
    z = me // MATES
    y = (me % MATES) // 2
    core = me % 2
    msg = cap * BLK
    base_extra = NZ * cap
    base_back = base_extra + 4 * extra
    base_in = base_back + NZ * back

    def more(n):
        return (n + core) % 2 == 0

    def at(dz, dy, dk, dx):
        ctx = ((z + dz) % PLANES) * MATES + ((y + dy) % 4) * 2 + (core + dk) % 2
        return (ctx, (x + dx) % HEADS)

    mates = [(dy, dk) for dy in range(4) for dk in range(2)][1:]

    def remote(src, dst, send, recv, device):
        return pltpu.make_async_remote_copy(
            src_ref=src, dst_ref=dst, send_sem=send, recv_sem=recv, device_id=device, device_id_type=MESH
        )

    def load(h, part):
        src = (q_hbm, k_hbm, v_hbm)[part].at[:, :, pl.ds(h * DH, DH)]
        return pltpu.make_async_copy(src, q_own.at[h] if part == 0 else kv_own.at[h, part - 1], load_sem.at[h, part])

    for part in range(3):
        for h in range(HEADS):
            load(h, part).start()
    own_w = pltpu.make_async_copy(
        w_hbm.at[:, pl.ds(pl.multiple_of(x * 512, 512), 512)], wg.at[0], w_sem.at[0, 0]
    )
    own_w.start()

    barrier = pltpu.get_barrier_semaphore()
    greet = [at(d, 0, 0, 0) for d in range(1, PLANES)]
    greet += [at(0, dy, dk, 0) for dy, dk in mates] + [at(0, 0, 0, d) for d in range(1, HEADS)]
    for device in greet:
        pl.semaphore_signal(barrier, inc=1, device_id=device, device_id_type=MESH)
    pl.semaphore_wait(barrier, len(greet))

    def w_copy(d):
        cols = pl.ds(pl.multiple_of(((x + d) % HEADS) * 512, 512), 512)
        return remote(w_hbm.at[:, cols], wg.at[HEADS - d], w_sem.at[0, d], w_sem.at[1, HEADS - d], at(0, 0, 0, d))

    def kv_near(h, dy):
        return remote(kv_own.at[h], kv_far.at[h, 2 * ((4 - dy) % 4)], ks_sem.at[h, dy], kr_sem.at[h, 2 * ((4 - dy) % 4)],
                      at(0, dy, 0, 0))

    def kv_next(h, part):
        dy, slot = (1, 6) if part == 0 else (3, 2)
        return remote(kv_far.at[h, slot, part], kv_far.at[h, 4, part], ks_sem.at[h, 4 + part],
                      kr_sem.at[h, 8 + part], at(0, dy, 0, 0))

    def kv_mate(h, dy):
        src = kv_own.at[h] if dy == 0 else kv_far.at[h, 2 * dy]
        return remote(src, kv_far.at[h, 2 * dy + 1], ks_sem.at[h, 6 + dy], kr_sem.at[h, 2 * dy + 1], at(0, 0, 1, 0))

    def near(out, into, send, recv, h, dy):
        slot = 2 * ((4 - dy) % 4) - 1
        return remote(out.at[h], into.at[h, slot], send.at[h, dy], recv.at[h, slot], at(0, dy, 0, 0))

    def mate(out, into, send, recv, h, dy):
        src = out.at[h] if dy == 0 else into.at[h, 2 * dy - 1]
        return remote(src, into.at[h, 2 * dy], send.at[h, 4 + dy], recv.at[h, 2 * dy], at(0, 0, 1, 0))

    def spread_start(arrays, h):
        mate(*arrays, h, 0).start()
        for dy in range(1, 4):
            near(*arrays, h, dy).start()

    def spread_finish(arrays, h):
        for dy in range(1, 4):
            near(*arrays, h, 4 - dy).wait_recv()
            mate(*arrays, h, dy).start()
        for dy in range(4):
            mate(*arrays, h, dy).wait_recv()

    def spread_drain(arrays, h):
        for dy in range(4):
            mate(*arrays, h, dy).wait_send()
        for dy in range(1, 4):
            near(*arrays, h, dy).wait_send()

    exc = (exc_out, exc_in, es_sem, er_sem)
    handed = (back_out, back_in, bs_sem, br_sem)

    def qx_copy(h, n):
        return remote(qx_out.at[h, n // 2], qx_in.at[h, n // 2, pl.ds(0, BLK)], qxs_sem.at[h, n // 2],
                      qxr_sem.at[h, n // 2], at(n + 1, 0, 0, 0))

    def ox_copy(h, n):
        return remote(qx_in.at[h, n // 2], ox_in.at[h, n // 2], oxs_sem.at[h, n // 2], oxr_sem.at[h, n // 2],
                      at(PLANES - 1 - n, 0, 0, 0))

    def q_copy(h, n):
        return remote(q_out.at[h, n], q_in.at[h, n, pl.ds(0, msg)], qs_sem.at[h, n], qr_sem.at[h, n], at(n + 1, 0, 0, 0))

    def o_copy(h, n):
        return remote(q_in.at[h, n], o_in.at[h, n], os_sem.at[h, n], or_sem.at[h, n], at(PLANES - 1 - n, 0, 0, 0))

    def x_copy(h, d):
        return remote(att.at[0, h], att.at[HEADS - d, h], xs_sem.at[h, d], xr_sem.at[h, HEADS - d], at(0, 0, 0, d))

    for h in range(HEADS):
        load(h, 0).wait()
    def spare_start(h):
        if spare:
            for e in range(spare):
                exc_out[h, e] = q_own[h, table[T_EXC + e]]
            spread_start(exc, h)

    def kv_start(h):
        src = k_hbm.at[:, :, pl.ds(0, DH)]
        for part in (1, 2):
            pltpu.make_async_copy(src, kv_own.at[h, part - 1], load_sem.at[h, part]).wait()

        @pl.loop(0, BLOCKS)
        def _(b):
            kv_own[h, 1, b] = kv_own[h, 1, b].T

        kv_near(h, 1).start()
        kv_near(h, 3).start()
        kv_mate(h, 0).start()

    def send_queries(h):
        @pl.loop(0, BLOCKS)
        def _(b):
            q_all[b] = q_own[h, b]

        if spare:
            spread_finish(exc, h)
            for n in range(NZ):
                for e in range(spare):
                    q_all[BLOCKS + n * spare + e] = exc_in[h, n, e]

        @pl.loop(0, NZ)
        def _(n):
            for i in range(cap):
                q_out[h, n, pl.ds(i * BLK, BLK), :] = q_all[table[T_SEND + n * 8 + i]]
            q_copy(h, n).start()
            if extra:
                @pl.when(more(n))
                def _():
                    qx_out[h, n // 2] = q_all[table[T_SEND + n * 8 + cap]]
                    qx_copy(h, n).start()

    spare_start(0)
    spare_start(1)
    kv_start(0)

    @pl.loop(0, 2)
    def _(h):
        send_queries(h)
        spare_start(h + 2)

    for d in range(1, HEADS):
        w_copy(d).start()

    def kv_first(h):
        for part, dy in ((0, 1), (1, 3)):
            kv_near(h, dy).wait_recv()
            kv_next(h, part).start()
            kv_mate(h, 4 - dy).start()

        @pl.when(h + 1 < HEADS)
        def _():
            kv_start(h + 1)

    def kv_last(h):
        kv_next(h, 0).wait_recv()
        kv_next(h, 1).wait_recv()
        kv_mate(h, 2).start()
        own = pltpu.make_async_copy(kv_own.at[h], kv_buf.at[:, pl.ds(0, BLOCKS)], kl_sem.at[0])
        own.start()
        copies = [
            pltpu.make_async_copy(kv_far.at[h, n], kv_buf.at[:, pl.ds(n * BLOCKS, BLOCKS)], kl_sem.at[n])
            for n in range(1, MATES)
        ]
        for dy in (1, 2, 3):
            copies[2 * dy - 1].start()
        for dy in range(4):
            kv_mate(h, dy).wait_recv()
            copies[2 * dy].start()
        own.wait()
        for copy in copies:
            copy.wait()

    def kv_block(number):
        return kv_buf[0, number], kv_buf[1, number]

    def far_blocks(h):
        @pl.loop(0, NZ)
        def _(n):
            q_copy(h, n).wait_recv()
            outs, tops = [], []
            for i in range(cap):
                query = q_in[h, n, pl.ds(i * BLK, BLK), :]
                out, top = attend(query, *kv_block(table[T_KEY + n * 8 + i]))
                outs.append(bf(out))
                tops.append(top)
            for i in range(cap):
                q_in[h, n, pl.ds(i * BLK, BLK), :] = outs[i]
            q_in[h, n, pl.ds(msg, 16), :] = split_logs(tops, cap)
            o_copy(h, n).start()
            if extra:
                @pl.when(more(n))
                def _():
                    qx_copy(h, n).wait_recv()
                    query = qx_in[h, n // 2, pl.ds(0, BLK), :]
                    out, top = attend(query, *kv_block(table[T_KEY + n * 8 + cap]))
                    qx_in[h, n // 2, pl.ds(0, BLK), :] = bf(out)
                    qx_in[h, n // 2, pl.ds(BLK, 16), :] = split_logs([top], 1)
                    ox_copy(h, n).start()

        for j in range(MATES):
            out, top = attend(q_own[h, table[T_IN_Q + j]], *kv_block(table[T_IN_K + j]))
            in_plane[h, j] = bf(out)
            logs[h, LOG_IN + j] = top

    def own_blocks(h):
        causal = lax.broadcasted_iota(jnp.int32, (BLK, BLK), 0) <= lax.broadcasted_iota(jnp.int32, (BLK, BLK), 1)

        @pl.loop(0, BLOCKS // 2)
        def _(pair):
            for half in range(2):
                b = pair * 2 + half
                out, top = attend(q_own[h, b], kv_own[h, 0, b], kv_own[h, 1, b], causal)
                own_out[b] = out
                own_log[b] = top

    def merge(h):
        @pl.loop(0, MATES)
        def _(j):
            o_all[base_in + j] = in_plane[h, j]

        @pl.loop(0, NZ)
        def _(n):
            o_copy(h, n).wait_recv()
            both = join_logs(o_in[h, n, pl.ds(msg, 16), :])
            for i in range(cap):
                o_all[n * cap + i] = o_in[h, n, pl.ds(i * BLK, BLK), :]
                logs[h, n * 8 + i] = both[i : i + 1]
            if extra:
                @pl.when(more(n))
                def _():
                    ox_copy(h, n).wait_recv()
                    o_all[base_extra + n // 2] = ox_in[h, n // 2, pl.ds(0, BLK), :]
                    logs[h, n * 8 + cap] = join_logs(ox_in[h, n // 2, pl.ds(BLK, 16), :])[0:1]

        if back:
            tops = []
            for f in range(back):
                back_out[h, pl.ds(f * BLK, BLK), :] = o_all[table[T_BACK + f]]
                tops.append(logs[h, table[T_BACK_LOG + f]])
            back_out[h, pl.ds(back * BLK, 16), :] = split_logs(tops, back)
            spread_start(handed, h)
            own_blocks(h)
            spread_finish(handed, h)
            for n in range(NZ):
                both = join_logs(back_in[h, n, pl.ds(back * BLK, 16), :])
                for f in range(back):
                    o_all[base_back + n * back + f] = back_in[h, n, pl.ds(f * BLK, BLK), :]
                    logs[h, LOG_BACK + n * 8 + f] = both[f : f + 1]
        else:
            own_blocks(h)

        @pl.loop(0, BLOCKS)
        def _(b):
            rows = pl.ds(pl.multiple_of(b * BLK, BLK), BLK)
            first = own_log[b]
            others, parts = [], []
            for j in range(2):
                item = b * 2 + j
                dead = (table[T_LIVE + item] - 1).astype(jnp.float32) * 1e30
                others.append(logs[h, table[T_LOG + item]] + dead)
                parts.append(o_all[table[T_OUT + item]].astype(jnp.float32))
            top = jnp.maximum(first, jnp.maximum(others[0], others[1]))
            weight = jnp.exp(first - top)
            total, merged = weight, weight * own_out[b]
            for other, part in zip(others, parts):
                weight = jnp.exp(other - top)
                total = total + weight
                merged = merged + weight * part
            att[0, h, rows, :] = bf(merged / total).T

        for d in range(1, HEADS):
            x_copy(h, d).start()

    def project(h):
        for d in range(1, HEADS):
            x_copy(h, d).wait_recv()
        weights = jnp.concatenate([wg[g, pl.ds(pl.multiple_of(h * DH, DH), DH), :] for g in range(HEADS)], axis=0)

        @pl.loop(0, ROWS // 256)
        def _(r):
            rows = pl.ds(pl.multiple_of(r * 256, 256), 256)
            left = jnp.concatenate([att[g, h, rows, :] for g in range(HEADS)], axis=1)
            acc[rows, :] = acc[rows, :] + jnp.dot(left, weights, preferred_element_type=jnp.float32)

    kv_first(0)

    @pl.loop(0, HEADS)
    def _(h):
        kv_last(h)

        @pl.when(h < 2)
        def _():
            send_queries(h + 2)

        far_blocks(h)

        @pl.when(h + 1 < HEADS)
        def _():
            kv_first(h + 1)

        @pl.when(h >= 1)
        def _():
            merge(h - 1)

    acc[...] = jnp.zeros_like(acc)
    own_w.wait()
    for d in range(1, HEADS):
        w_copy(d).wait_recv()

    project(0)
    project(1)
    merge(HEADS - 1)
    project(2)
    project(3)

    @pl.loop(0, ROWS // 256)
    def _(r):
        rows = pl.ds(pl.multiple_of(r * 256, 256), 256)
        o_ref[rows, :] = bf(acc[rows, :])

    for d in range(1, HEADS):
        w_copy(d).wait_send()

    @pl.loop(0, HEADS)
    def _(h):
        kv_near(h, 1).wait_send()
        kv_near(h, 3).wait_send()
        for part in range(2):
            kv_next(h, part).wait_send()
        for dy in range(4):
            kv_mate(h, dy).wait_send()
        for n in range(NZ):
            q_copy(h, n).wait_send()
            o_copy(h, n).wait_send()
            if extra:
                @pl.when(more(n))
                def _():
                    qx_copy(h, n).wait_send()
                    ox_copy(h, n).wait_send()
        if spare:
            spread_drain(exc, h)
        if back:
            spread_drain(handed, h)
        for d in range(1, HEADS):
            x_copy(h, d).wait_send()


def layer(sizes, number, table, queries, keys, values, out_weight):
    cap, extra, spare, back = sizes
    msg = cap * BLK
    tile = (BLK, DH)
    few = 4 if extra else 1
    b16 = jnp.bfloat16
    dma = pltpu.SemaphoreType.DMA
    any_space = pl.BlockSpec(memory_space=pl.ANY)
    out, _ = pl.pallas_call(
        functools.partial(layer_kernel, cap, extra, spare, back),
        name=f"layer_{cap}_{extra}",
        out_shape=(
            jax.ShapeDtypeStruct((ROWS, 512), b16),
            jax.ShapeDtypeStruct((HEADS, MATES, 2, BLOCKS) + tile, b16),
        ),
        in_specs=[pl.BlockSpec(memory_space=pltpu.SMEM)] + [any_space] * 4,
        out_specs=(pl.BlockSpec(memory_space=pltpu.VMEM), any_space),
        scratch_shapes=[
            pltpu.VMEM((HEADS, BLOCKS) + tile, b16),
            pltpu.VMEM((BLOCKS + NZ * spare,) + tile, b16),
            pltpu.VMEM((HEADS, 2, BLOCKS) + tile, b16),
            pltpu.VMEM((HEADS, NZ, msg, DH), b16),
            pltpu.VMEM((HEADS, NZ, msg + 16, DH), b16),
            pltpu.VMEM((HEADS, NZ, msg + 16, DH), b16),
            pltpu.VMEM((HEADS, few, BLK, DH), b16),
            pltpu.VMEM((HEADS, few, BLK + 16, DH), b16),
            pltpu.VMEM((HEADS, few, BLK + 16, DH), b16),
            pltpu.VMEM((NZ * (cap + back) + 4 * extra + MATES,) + tile, b16),
            pltpu.VMEM((HEADS, max(spare, 1)) + tile, b16),
            pltpu.VMEM((HEADS, NZ, max(spare, 1)) + tile, b16),
            pltpu.VMEM((HEADS, back * BLK + 16, DH), b16),
            pltpu.VMEM((HEADS, NZ, back * BLK + 16, DH), b16),
            pltpu.VMEM((HEADS, MATES) + tile, b16),
            pltpu.VMEM((2, MATES * BLOCKS) + tile, b16),
            pltpu.VMEM((BLOCKS,) + tile, jnp.float32),
            pltpu.VMEM((BLOCKS, 1, DH), jnp.float32),
            pltpu.VMEM((HEADS, 120, 1, DH), jnp.float32),
            pltpu.VMEM((HEADS, HEADS, ROWS, DH), b16),
            pltpu.VMEM((HEADS, 512, 512), b16),
            pltpu.VMEM((ROWS, 512), jnp.float32),
            dma((HEADS, 3)), dma((2, HEADS)),
            dma((HEADS, NZ)), dma((HEADS, NZ)), dma((HEADS, NZ)), dma((HEADS, NZ)),
            dma((HEADS, 4)), dma((HEADS, 4)), dma((HEADS, 4)), dma((HEADS, 4)),
            dma((HEADS, 8)), dma((HEADS, NZ)), dma((HEADS, 8)), dma((HEADS, NZ)),
            dma((HEADS, 10)), dma((HEADS, 10)), dma((MATES,)),
            dma((HEADS, HEADS)), dma((HEADS, HEADS)),
        ],
        compiler_params=pltpu.CompilerParams(
            collective_id=number, has_side_effects=True, vmem_limit_bytes=63 << 20
        ),
    )(table, *[array.reshape(BLOCKS, BLK, -1) for array in (queries, keys, values)], out_weight)
    return out


def swap_kernel(mine, out, every, send_sem, recv_sem):
    me = lax.axis_index("ctx")
    x = lax.axis_index("head")
    z, w = me // MATES, me % MATES
    planes = [((z + d) % PLANES * MATES + w, x) for d in range(1, PLANES)]
    mates = [(z * MATES + (w + d) % MATES, x) for d in range(1, MATES)]
    barrier = pltpu.get_barrier_semaphore()
    for device in planes + mates:
        pl.semaphore_signal(barrier, inc=1, device_id=device, device_id_type=MESH)
    pl.semaphore_wait(barrier, len(planes + mates))
    every[w, z] = mine[...]
    for stage, devices, part in ((0, planes, every.at[w, z]), (1, mates, every.at[w])):
        copies = [
            pltpu.make_async_remote_copy(
                src_ref=part, dst_ref=part, send_sem=send_sem.at[stage, n], recv_sem=recv_sem.at[stage, n],
                device_id=device, device_id_type=MESH,
            )
            for n, device in enumerate(devices)
        ]
        for copy in copies:
            copy.start()
        for copy in copies:
            copy.wait()
    out[...] = every[...]


def swap(mine):
    vmem = pl.BlockSpec(memory_space=pltpu.VMEM)
    shape = (MATES, PLANES, 1, DH)
    return pl.pallas_call(
        swap_kernel,
        name="swap",
        out_shape=jax.ShapeDtypeStruct(shape, jnp.int32),
        in_specs=[vmem],
        out_specs=vmem,
        scratch_shapes=[
            pltpu.VMEM(shape, jnp.int32), pltpu.SemaphoreType.DMA((2, 7)), pltpu.SemaphoreType.DMA((2, 7))
        ],
        compiler_params=pltpu.CompilerParams(collective_id=3, has_side_effects=True),
    )(mine)


def total(mask, value, axes):
    return jnp.sum(jnp.where(mask, value, 0), axis=axes)


def room_of(cap, extra):
    eight = jnp.arange(8, dtype=jnp.int32)
    step = (eight - eight[:, None, None]) % 8 - 1
    more = (step + eight[None, :, None]) % 2 == 0
    return jnp.where(more, cap + extra, cap)


def route(places, cap, extra, spare, back):
    eight = jnp.arange(8, dtype=jnp.int32)
    item = jnp.arange(32, dtype=jnp.int32)
    plane = jnp.where(places >= 0, places // 128, -1)
    source = eight[:, None, None]
    goes = plane[..., None] == eight
    away = (plane >= 0) & (plane != source)
    count = jnp.sum(goes, axis=2, dtype=jnp.int32)
    earlier = item[None, :] < item[:, None]
    rank = jnp.sum((plane[..., None, :] == plane[..., :, None]) & earlier, axis=-1, dtype=jnp.int32)
    limit = room_of(cap, extra)
    own_limit = total(goes, limit[:, :, None, :], -1)
    over = away & (rank >= own_limit)
    spare_rank = jnp.sum(over[..., None, :] & earlier, axis=-1, dtype=jnp.int32)
    apart = eight[:, None, None] != eight
    over_count = jnp.where(apart, jnp.maximum(count - limit, 0), 0)
    room = jnp.where(apart, jnp.maximum(limit - count, 0), 0)
    before = eight[None, :] < eight[:, None]
    over_before = total(before[None, :, :, None], over_count[:, None], 2)
    order = (eight[:, None] - eight[None, :]) % 8
    first = order[None, :, :] < order[:, None, :]
    room_before = total(first[None], room[:, None], 2)
    turn = total(goes, over_before[:, :, None, :], -1) + rank - own_limit
    mine = goes[:, :, :, None, :]
    low = total(mine, room_before[:, None, None], -1)
    size = total(mine, room[:, None, None], -1)
    filled = total(mine, count[:, None, None], -1)
    turn8 = turn[..., None]
    hit = over[..., None] & (low <= turn8) & (turn8 < low + size)
    carrier = jnp.where(over, total(hit, eight, -1), eight[None, :, None])
    slot = jnp.where(over, total(hit, filled + turn8 - low, -1), rank)
    flat_over, flat_carrier = over.reshape(8, 256), jnp.where(over, carrier, -1).reshape(8, 256)
    flat = jnp.arange(256, dtype=jnp.int32)
    same = flat_over[:, None, :] & (flat_carrier[:, None, :] == flat_carrier[:, :, None])
    back_rank = jnp.sum(same & (flat[None, :] < flat[:, None]), axis=-1, dtype=jnp.int32).reshape(8, 8, 32)
    fits = ~over | (jnp.any(hit, axis=-1) & (spare_rank < spare) & (back_rank < back))
    return plane, rank, over, spare_rank, carrier, slot, back_rank, jnp.all(fits)


def make_table(places, routed, me, cap, extra, spare, back):
    plane, rank, over, spare_rank, carrier, slot, back_rank, _ = routed
    eight = jnp.arange(8, dtype=jnp.int32)
    item = jnp.arange(32, dtype=jnp.int32)
    z, w = me // 8, me % 8

    def relative(device):
        return ((device // 2 - w // 2) % 4) * 2 + (device - w) % 2

    def here(array):
        return lax.dynamic_index_in_dim(array, z, 0, keepdims=False)

    def own(array):
        return lax.dynamic_index_in_dim(here(array), w, 0, keepdims=False)

    shift = jnp.arange(7, dtype=jnp.int32)[:, None, None, None]
    step = (plane - z) % 8 - 1
    key = relative((places % 128) // 16) * 16 + places % 16

    plane_h, over_h, spare_h, carrier_h, slot_h, back_h, step_h = map(
        here, (plane, over, spare_rank, carrier, slot, back_rank, step)
    )
    sent = (plane_h >= 0) & (plane_h != z) & (carrier_h == w)
    source = jnp.where(
        eight[:, None] == w, item[None, :] // 2, 16 + (relative(eight)[:, None] - 1) * spare + spare_h
    )
    slots = eight[None, :, None, None]
    send = total(sent & (step_h == shift) & (slot_h == slots), source, (-1, -2))
    comes = (plane == z) & (eight[:, None, None] != z) & (carrier == w)
    from_step = ((z - eight) % 8 - 1)[:, None, None]
    arrive = total(comes & (from_step == shift[..., None]) & (slot == slots[..., None]), key, (-1, -2, -3))

    plane_o, over_o, spare_o, carrier_o, slot_o, back_o, step_o, rank_o, key_o = map(
        own, (plane, over, spare_rank, carrier, slot, back_rank, step, rank, key)
    )
    exc = total(over_o & (spare_o == eight[:, None]), item // 2, -1)
    inside = plane_o == z
    local = inside & (rank_o == eight[:, None])
    in_q = total(local, item // 2, -1)
    in_k = total(local, key_o, -1)
    rel = relative(carrier_o) - 1
    def far_place(step, slot):
        return jnp.where(slot == cap, 7 * cap + step // 2, step * cap + slot)

    base_back = 7 * cap + 4 * extra
    place = jnp.where(over_o, base_back + rel * back + back_o, far_place(step_o, slot_o))
    place = jnp.where(inside, base_back + 7 * back + rank_o, place)
    log = jnp.where(over_o, LOG_BACK + rel * 8 + back_o, step_o * 8 + slot_o)
    log = jnp.where(inside, LOG_IN + rank_o, log)
    live = plane_o >= 0
    place, log = jnp.where(live, place, 0), jnp.where(live, log, 0)
    foreign = over_h & (carrier_h == w) & (back_h == eight[:, None, None])
    back_place = total(foreign, far_place(step_h, slot_h), (-1, -2))
    back_log = total(foreign, step_h * 8 + slot_h, (-1, -2))
    pieces = [send.reshape(-1), arrive.reshape(-1), exc, in_q, in_k, place, log, live, back_place, back_log]
    return jnp.concatenate([piece.astype(jnp.int32) for piece in pieces])


def shards(queries, keys, values, out_weight, block_order, selection):
    me = lax.axis_index("ctx")
    stored = jnp.arange(block_order.shape[0], dtype=jnp.int32)
    wanted = selection.reshape(-1)
    own_ids = lax.dynamic_slice_in_dim(block_order, me * BLOCKS, BLOCKS)
    where_stored = total(wanted[:, None] == block_order[None, :], stored[None, :], -1)
    mine = jnp.where(wanted != jnp.repeat(own_ids, 2), where_stored, -1)
    every = swap(jnp.pad(mine, (0, DH - mine.shape[0])).reshape(1, DH))
    places = jnp.swapaxes(every[:, :, 0, :32], 0, 1)
    arrays = (queries, keys, values, out_weight)
    eight = jnp.arange(8, dtype=jnp.int32)
    count = jnp.sum((places // 128)[..., None] == eight, axis=2, dtype=jnp.int32)
    count = jnp.where(eight[:, None, None] != eight, count, 0)
    many = jnp.sum(count, axis=1) > 8 * SIZES[0][0]
    over = jnp.sum(jnp.maximum(count - SIZES[0][0], 0), axis=2) > SIZES[0][2]
    extra = (jnp.any(many) | jnp.any(over)).astype(jnp.int32)
    routed = route(places, SIZES[0][0], extra, *SIZES[0][2:])

    def variant(number):
        def run():
            sizes = SIZES[number]
            used = route(places, *sizes) if number == 2 else routed
            return layer(sizes, number, make_table(places, used, me, *sizes), *arrays)

        return run

    return lax.switch(jnp.where(routed[-1], extra, 2), [variant(number) for number in range(3)])


def solution(mesh):
    return jax.shard_map(
        shards,
        mesh=mesh,
        in_specs=(
            P("ctx", "head"),
            P("ctx", "head"),
            P("ctx", "head"),
            P("head", None),
            P(),
            P("ctx", None),
        ),
        out_specs=P("ctx", "head"),
        check_vma=False,
    )
```
